256 devices in a mesh: ctx: 64 (over z, y, core), dp: 4 (over x).
Axes of the slice: x: 4, y: 4, z: 8, core: 2. Of those that a mesh axis runs over, the one named last changes fastest.
Arguments:
- queries: bfloat16 [32768, 2048], P(('dp', 'ctx')), parts along dimension 0, may hold values from -6 to 6
- keys: bfloat16 [32768, 512], P(('dp', 'ctx')), parts along dimension 0, may hold values from -6 to 6
- values: bfloat16 [32768, 512], P(('dp', 'ctx')), parts along dimension 0, may hold values from -6 to 6
- outputs: bfloat16 [32768, 2048], P(('dp', 'ctx')), parts along dimension 0, may hold values from -6 to 6
- out_grad: bfloat16 [32768, 2048], P(('dp', 'ctx')), parts along dimension 0, may hold values from -6 to 6
- log_sum_exp: float32 [16, 32768], P(None, ('dp', 'ctx')), parts along dimension 1
- spans: int32 [16], P('dp'), parts along dimension 0, may hold values from 257 to 8192, as said below
Outputs:
- grad_queries: bfloat16 [32768, 2048], P(('dp', 'ctx')), parts along dimension 0
- grad_keys: bfloat16 [32768, 512], P(('dp', 'ctx')), parts along dimension 0
- grad_values: bfloat16 [32768, 512], P(('dp', 'ctx')), parts along dimension 0
The draws below stay inside these ranges and needn't reach their ends.
There are 4 independent parts, one for each index of `dp`. The reference program is written for one: setup_inputs(seed, part) draws one part's arguments, and reference() takes and returns one part's arrays. A program takes and returns all parts, laid end to end along the dimension named above; each array names one. Nothing has to cross between parts.
Inputs may be any that keep to these rules, and one draw needn't show every extreme that they name: `spans`: in some order, one key-value head has a span above 256 and at most 512, one above 1024 and at most 2048, one above 2048 and at most 4096, and one exactly 8192.
All inputs are finite; a program needn't handle non-finite values.
Results may differ from the reference program's by a relative error of at most 0.0058.
Values may be sent and summed in bfloat16 or wider, within the bound.
A program may use at most 64 MiB of HBM per device.

```python
import math
import jax
import jax.numpy as jnp
from jax import lax

Q_HEADS = 16
KV_HEADS = 4
HEAD_DIM = 128
SEQ = 8192
SPAN_SHORT = 512
SPAN_MID = 2048
SPAN_HALF = 4096


def class_spans(key):
    order = jax.random.permutation(jax.random.fold_in(key, 1), KV_HEADS)
    tops = jnp.array([SPAN_SHORT, SPAN_MID, SPAN_HALF, SEQ], jnp.int32)
    halves = jnp.array([SPAN_SHORT // 2, SPAN_MID // 2, SPAN_HALF // 2, 1], jnp.int32)
    keeps = jnp.array([1, 1, 1, 0], jnp.int32)
    raw = jax.random.randint(jax.random.fold_in(key, 2), (KV_HEADS,), 0, 1048576, jnp.int32)
    cuts = raw % halves * keeps
    return (tops - cuts)[order]


def draw_spans(key, part):
    return class_spans(key)


def draw_log_sum_exp(key, part):
    shared = class_spans(key)
    key = jax.random.fold_in(key, 7)
    per_query = jnp.repeat(shared, Q_HEADS // KV_HEADS)
    places = jnp.arange(SEQ, dtype=jnp.int32)
    counted = jnp.minimum(per_query[:, None], places[None, :] + 1).astype(jnp.float32)
    extra = jax.random.uniform(key, (Q_HEADS, SEQ), jnp.float32, 0.0, 1.0)
    return jnp.log(counted) + extra


def level_of(key, dims, pieces, smallest, top_value):
    factor_of, own = 1.0, jax.random.fold_in(key, 6)
    for position, blocks in pieces:
        draws = jnp.exp(jax.random.uniform(jax.random.fold_in(own, position), (blocks,), jnp.float32, smallest / len(pieces), top_value / len(pieces)))
        factor_of = factor_of * jnp.repeat(draws, dims[position] // blocks).reshape([-1 if axis == position else 1 for axis in range(len(dims))])
    return factor_of


def centred(own_key, dims, width, bound, cuts=(), held_as=jnp.bfloat16):
    gain = level_of(own_key, dims, cuts, -0.22, 0.18) if cuts else 1.0
    values = jax.random.normal(own_key, dims, jnp.float32) * width * gain
    return jnp.minimum(jnp.maximum(values, -bound), bound).astype(held_as)


def setup_inputs(seed: int = 0, part: int = 0) -> dict:
    arg_keys = jax.random.split(jax.random.key(seed), 8)
    part_keys = jax.random.split(jax.random.fold_in(arg_keys[7], part), 8)
    queries = centred(part_keys[0], (SEQ, Q_HEADS * HEAD_DIM), 1.0, 6.0, ((0, 64),))
    keys = centred(part_keys[1], (SEQ, KV_HEADS * HEAD_DIM), 1.0, 6.0, ((0, 64),))
    values = centred(part_keys[2], (SEQ, KV_HEADS * HEAD_DIM), 1.0, 6.0, ((0, 64),))
    outputs = centred(part_keys[3], (SEQ, Q_HEADS * HEAD_DIM), 0.5, 6.0, ((0, 64),))
    out_grad = centred(part_keys[4], (SEQ, Q_HEADS * HEAD_DIM), 1.0, 6.0, ((0, 64),))
    log_sum_exp = draw_log_sum_exp(jax.random.fold_in(jax.random.fold_in(arg_keys[7], part), 71), part)
    spans = draw_spans(jax.random.fold_in(jax.random.fold_in(arg_keys[7], part), 71), part)
    return {"queries": queries, "keys": keys, "values": values, "outputs": outputs, "out_grad": out_grad, "log_sum_exp": log_sum_exp, "spans": spans}


def reference(queries, keys, values, outputs, out_grad, log_sum_exp, spans):
    group = Q_HEADS // KV_HEADS
    scaling = 1.0 / math.sqrt(HEAD_DIM)
    block = min(512, SEQ)
    query_all = queries.reshape(SEQ, Q_HEADS, HEAD_DIM)
    grad_all = out_grad.reshape(SEQ, Q_HEADS, HEAD_DIM)
    delta_all = lax.optimization_barrier(jnp.sum(out_grad.astype(jnp.float32).reshape(SEQ, Q_HEADS, HEAD_DIM) * outputs.astype(jnp.float32).reshape(SEQ, Q_HEADS, HEAD_DIM), axis=2))
    query_heads = []
    key_heads = []
    value_heads = []
    for key_head in range(KV_HEADS):
        span_value = spans[key_head]
        low_head = key_head * group
        key_rows = keys[:, key_head * HEAD_DIM:(key_head + 1) * HEAD_DIM].astype(jnp.float32)
        value_rows = values[:, key_head * HEAD_DIM:(key_head + 1) * HEAD_DIM].astype(jnp.float32)
        key_total = jnp.zeros((SEQ, HEAD_DIM), jnp.float32)
        value_total = jnp.zeros((SEQ, HEAD_DIM), jnp.float32)
        query_blocks = []
        for first in range(0, SEQ, block):
            last = first + block
            query_rows = query_all[first:last, low_head:low_head + group].astype(jnp.float32)
            grad_rows = grad_all[first:last, low_head:low_head + group].astype(jnp.float32)
            lse_rows = log_sum_exp[low_head:low_head + group, first:last]
            delta_rows = delta_all[first:last, low_head:low_head + group].T
            scores = jnp.einsum('bgd,sd->gbs', query_rows, key_rows[:last]) * scaling
            row_index = first + jnp.arange(block, dtype=jnp.int32)
            col_index = jnp.arange(last, dtype=jnp.int32)
            distance = row_index[:, None] - col_index[None, :]
            allowed = (distance >= 0) & (distance < span_value)
            probability = jnp.exp(jnp.where(allowed[None], scores - lse_rows[:, :, None], -1e+30))
            rounded = probability.astype(jnp.bfloat16).astype(jnp.float32)
            dprobs = jnp.einsum('bgd,sd->gbs', grad_rows, value_rows[:last])
            dscores = (probability * (dprobs - delta_rows[:, :, None]) * scaling).astype(jnp.bfloat16).astype(jnp.float32)
            query_blocks.append(jnp.einsum('gbs,sd->bgd', dscores, key_rows[:last]))
            key_total = key_total.at[:last].add(jnp.einsum('gbs,bgd->sd', dscores, query_rows))
            value_total = value_total.at[:last].add(jnp.einsum('gbs,bgd->sd', rounded, grad_rows))
        query_heads.append(jnp.concatenate(query_blocks, axis=0))
        key_heads.append(key_total)
        value_heads.append(value_total)
    grad_queries = jnp.concatenate(query_heads, axis=1).reshape(SEQ, Q_HEADS * HEAD_DIM).astype(jnp.bfloat16)
    grad_keys = jnp.concatenate(key_heads, axis=1).astype(jnp.bfloat16)
    grad_values = jnp.concatenate(value_heads, axis=1).astype(jnp.bfloat16)
    return (grad_queries, grad_keys, grad_values)
```

```python
import functools
import math

import jax
import jax.numpy as jnp
from jax import lax
from jax.experimental import pallas as pl
from jax.experimental.pallas import tpu as pltpu
from jax.sharding import PartitionSpec as P

Q_HEADS = 16
KV_HEADS = 4
GROUP = 4
HEAD_DIM = 128
PLANES = 8
COLUMNS = 4
ROWS = 128
SCALING = 1.0 / math.sqrt(HEAD_DIM)
LOG2E = math.log2(math.e)
BF16 = jnp.bfloat16
F32 = jnp.float32
MESH = pl.DeviceIdType.MESH
NT = (((1,), (1,)), ((), ()))
NN = (((1,), (0,)), ((), ()))
FAR = ((7, 1), (4, 2))


def dot(a, b, dims=NN):
    return lax.dot_general(a, b, dims, preferred_element_type=F32)


def far_of(core, slot):
    return jnp.where(core == 0, FAR[0][slot], FAR[1][slot])


def pack_kernel(heads, q_ref, g_ref, o_ref, k_ref, v_ref, lse_ref, qd_ref, kv_ref, st_ref):
    head = heads[pl.program_id(0) * 2 + pl.program_id(1)]
    st_ref[0, 0] = jnp.zeros((8, 256), F32)
    for g in range(GROUP):
        cols = slice(g * HEAD_DIM, (g + 1) * HEAD_DIM)
        qd_ref[0, 0, 0, g] = q_ref[:, cols]
        qd_ref[0, 0, 1, g] = g_ref[:, cols]
        product = g_ref[:, cols].astype(F32) * o_ref[:, cols].astype(F32)
        delta = jnp.sum(product.T, axis=0, keepdims=True)
        lanes = slice((g % 2) * ROWS, (g % 2 + 1) * ROWS)
        lse = lse_ref[pl.ds(head * GROUP + g, 1), :]
        st_ref[0, 0, g // 2 : g // 2 + 1, lanes] = lse * LOG2E
        st_ref[0, 0, 2 + g // 2 : 3 + g // 2, lanes] = delta
    kv_ref[0, 0, 0] = k_ref[...]
    kv_ref[0, 0, 1] = v_ref[...]


def pack(heads, queries, out_grad, outputs, keys, values, log_sum_exp):
    wide = pl.BlockSpec((ROWS, GROUP * HEAD_DIM), lambda r, s, h: (0, h[r * 2 + s]))
    narrow = pl.BlockSpec((ROWS, HEAD_DIM), lambda r, s, h: (0, h[r * 2 + s]))
    return pl.pallas_call(
        pack_kernel,
        grid_spec=pltpu.PrefetchScalarGridSpec(
            num_scalar_prefetch=1,
            grid=(2, 2),
            in_specs=[wide, wide, wide, narrow, narrow, pl.BlockSpec((Q_HEADS, ROWS), lambda r, s, h: (0, 0))],
            out_specs=[
                pl.BlockSpec((1, 1, 2, GROUP, ROWS, HEAD_DIM), lambda r, s, h: (r, s, 0, 0, 0, 0)),
                pl.BlockSpec((1, 1, 2, ROWS, HEAD_DIM), lambda r, s, h: (r, s, 0, 0, 0)),
                pl.BlockSpec((1, 1, 8, 256), lambda r, s, h: (r, s, 0, 0)),
            ],
        ),
        out_shape=[
            jax.ShapeDtypeStruct((2, 2, 2, GROUP, ROWS, HEAD_DIM), BF16),
            jax.ShapeDtypeStruct((2, 2, 2, ROWS, HEAD_DIM), BF16),
            jax.ShapeDtypeStruct((2, 2, 8, 256), F32),
        ],
        name="pack",
    )(heads, queries, out_grad, outputs, keys, values, log_sum_exp)


def place():
    me = lax.axis_index("ctx")
    return me // 8, (me // 2) % 4, me % 2


def at(z, y, core):
    return {"ctx": z * 8 + y * 2 + core}


def remote(src, dst, send, recv, device):
    return pltpu.make_async_remote_copy(
        src_ref=src, dst_ref=dst, send_sem=send, recv_sem=recv, device_id=device, device_id_type=MESH
    )


def greet(z, y, core):
    barrier = pltpu.get_barrier_semaphore()
    count = 1
    pl.semaphore_signal(barrier, inc=1, device_id=at(z, y, 1 - core), device_id_type=MESH)
    for c in range(2):
        for dy in range(1, COLUMNS):
            pl.semaphore_signal(barrier, inc=1, device_id=at(z, (y + dy) % 4, c), device_id_type=MESH)
            count += 1
        for dz in range(1, PLANES):
            pl.semaphore_signal(barrier, inc=1, device_id=at((z + dz) % 8, y, c), device_id_type=MESH)
            count += 1
    pl.semaphore_wait(barrier, count)


def spread_kernel(qd_ref, kv_ref, st_ref, qd_all, kv_all, st_all, local, s_sib, s_y, s_fw, s_z, r_q, r_s, r_kv):
    z, y, core = place()
    greet(z, y, core)
    other = 1 - core
    mine = [
        pltpu.make_async_copy(qd_ref.at[0], qd_all.at[y, core], local.at[0]),
        pltpu.make_async_copy(st_ref.at[0], st_all.at[y, core], local.at[1]),
        pltpu.make_async_copy(kv_ref.at[0], kv_all.at[0, core], local.at[2]),
    ]
    for c in mine:
        c.start()
    sends = []
    for role in range(2):
        target = core if role == 0 else other
        for step, dy in enumerate((1, 3)):
            to = at(z, (y + dy) % 4, target)
            for slot in range(2):
                sends.append(
                    remote(
                        qd_ref.at[role, slot],
                        qd_all.at[y, core, slot],
                        s_y.at[role, step, slot],
                        r_q.at[y, core, slot],
                        to,
                    )
                )
            sends.append(remote(st_ref.at[role], st_all.at[y, core], s_y.at[role, step, 2], r_s.at[y, core], to))
    to = at(z, y, other)
    for slot in range(2):
        sends.append(remote(qd_ref.at[1, slot], qd_all.at[y, core, slot], s_sib.at[slot], r_q.at[y, core, slot], to))
        sends.append(
            remote(kv_ref.at[1, slot], kv_all.at[0, core, slot], s_sib.at[2 + slot], r_kv.at[0, core, slot], to)
        )
    sends.append(remote(st_ref.at[1], st_all.at[y, core], s_sib.at[4], r_s.at[y, core], to))
    for c in sends:
        c.start()

    def keys_to(d, slot, role):
        target = core if role == 0 else other
        return remote(
            kv_ref.at[role, slot],
            kv_all.at[d, core, slot],
            s_z.at[d, role, slot],
            r_kv.at[d, core, slot],
            at((z + d) % 8, y, target),
        )

    def each_key_send(act):
        for d in range(1, PLANES):
            for role in range(2):
                target = core if role == 0 else other
                for slot in range(2):
                    if d <= max(FAR[0][slot], FAR[1][slot]):

                        @pl.when((z + d < PLANES) & (d <= far_of(target, slot)))
                        def _(d=d, slot=slot, role=role):
                            act(keys_to(d, slot, role))

    each_key_send(lambda c: c.start())

    def landed(col, c, slot):
        return remote(qd_ref.at[0, slot], qd_all.at[col, c, slot], s_sib.at[0], r_q.at[col, c, slot], to)

    def landed_st(col, c):
        return remote(st_ref.at[0], st_all.at[col, c], s_sib.at[0], r_s.at[col, c], to)

    forwards = []
    before, after, across = (y + 3) % 4, (y + 1) % 4, (y + 2) % 4
    for c in range(2):
        landed(before, c, 0).wait_recv()
        landed_st(before, c).wait_recv()
        up = at(z, after, core)
        forwards.append(
            remote(qd_all.at[before, c, 0], qd_all.at[before, c, 0], s_fw.at[c, 0], r_q.at[before, c, 0], up)
        )
        forwards.append(remote(st_all.at[before, c], st_all.at[before, c], s_fw.at[c, 1], r_s.at[before, c], up))
        forwards[-2].start()
        forwards[-1].start()
        landed(after, c, 1).wait_recv()
        down = at(z, before, core)
        forwards.append(
            remote(qd_all.at[after, c, 1], qd_all.at[after, c, 1], s_fw.at[c, 2], r_q.at[after, c, 1], down)
        )
        forwards[-1].start()
    for c in range(2):
        landed(before, c, 1).wait_recv()
        landed(after, c, 0).wait_recv()
        landed_st(after, c).wait_recv()
        landed(across, c, 0).wait_recv()
        landed(across, c, 1).wait_recv()
        landed_st(across, c).wait_recv()
    for slot in range(2):
        landed(y, other, slot).wait_recv()
    landed_st(y, other).wait_recv()

    def keys_landed(d, c, slot):
        return remote(kv_ref.at[0, slot], kv_all.at[d, c, slot], s_sib.at[0], r_kv.at[d, c, slot], to)

    for slot in range(2):
        keys_landed(0, other, slot).wait_recv()
        for d in range(1, max(FAR[0][slot], FAR[1][slot]) + 1):

            @pl.when((z >= d) & (d <= far_of(core, slot)))
            def _(d=d, slot=slot):
                for c in range(2):
                    keys_landed(d, c, slot).wait_recv()

    for c in mine:
        c.wait()
    for c in sends + forwards:
        c.wait_send()
    each_key_send(lambda c: c.wait_send())


def spread(qd, kv, st):
    anywhere = pl.BlockSpec(memory_space=pl.ANY)
    dma = pltpu.SemaphoreType.DMA
    return pl.pallas_call(
        spread_kernel,
        in_specs=[anywhere] * 3,
        out_specs=[anywhere] * 3,
        out_shape=[
            jax.ShapeDtypeStruct((COLUMNS, 2, 2, 2, GROUP, ROWS, HEAD_DIM), BF16),
            jax.ShapeDtypeStruct((PLANES, 2, 2, 2, ROWS, HEAD_DIM), BF16),
            jax.ShapeDtypeStruct((COLUMNS, 2, 2, 8, 256), F32),
        ],
        scratch_shapes=[
            dma((3,)),
            dma((5,)),
            dma((2, 2, 3)),
            dma((2, 3)),
            dma((PLANES, 2, 2)),
            dma((COLUMNS, 2, 2)),
            dma((COLUMNS, 2)),
            dma((PLANES, 2, 2)),
        ],
        compiler_params=pltpu.CompilerParams(collective_id=0, has_side_effects=True),
        name="spread",
    )(qd, kv, st)


def grads_kernel(info, qd_ref, kv_ref, st_ref, dq_ref, dkv_ref, dq_acc, dkv_acc):
    z, y = info[0], info[1]
    dkv_acc[...] = jnp.zeros_like(dkv_acc)

    def tile(slot, col, d0, count, span, masked):
        size = count * 256
        k = kv_ref[pl.ds(d0, count), :, slot, 0].reshape(size, HEAD_DIM)
        v = kv_ref[pl.ds(d0, count), :, slot, 1].reshape(size, HEAD_DIM)
        k_t = k.T
        for half in range(2):
            for pair in range(2):
                heads = slice(2 * pair, 2 * pair + 2)
                q = qd_ref[col, half, slot, 0, heads].reshape(256, HEAD_DIM)
                g = qd_ref[col, half, slot, 1, heads].reshape(256, HEAD_DIM)
                lse = st_ref[col, half, slot, pair : pair + 1]
                delta = st_ref[col, half, slot, 2 + pair : 3 + pair]
                prob = jnp.exp2(dot(k, q, NT) * (SCALING * LOG2E) - lse)
                if masked:
                    key = lax.broadcasted_iota(jnp.int32, (size, 256), 0)
                    row = lax.broadcasted_iota(jnp.int32, (size, 256), 1) % ROWS
                    distance = row - key + (d0 * 1024 + (col - y) * 256 + half * ROWS)
                    prob = jnp.where((distance >= 0) & (distance < span), prob, 0.0)
                ds = (prob * (dot(v, g, NT) - delta)).astype(BF16)
                low = prob.astype(BF16)
                dkv_acc[slot, 0, pl.ds(d0, count)] += dot(ds, q).reshape(count, 256, HEAD_DIM)
                dkv_acc[slot, 1, pl.ds(d0, count)] += dot(low, g).reshape(count, 256, HEAD_DIM)
                dq_acc[half, pair] += dot(k_t, ds)

    for slot in range(2):
        span = info[2 + slot]

        def column(col, carry, slot=slot, span=span):
            dq_acc[...] = jnp.zeros_like(dq_acc)
            ahead = col - y
            low = jnp.where(ahead >= 0, 0, 1)
            high = jnp.minimum(z, ((span + 254) // 256 - ahead + 4) // 4 - 1)
            full_low = jnp.where(ahead > 0, 0, 1)
            full_high = jnp.minimum(z, ((span - 256) // 256 - ahead + 4) // 4 - 1)
            full_count = jnp.maximum(full_high - full_low + 1, 0)

            def edge(d, c):
                tile(slot, col, d, 1, span, True)
                return c

            lax.fori_loop(low, jnp.minimum(full_low, high + 1), edge, 0)
            lax.fori_loop(jnp.maximum(full_low + full_count, low), high + 1, edge, 0)
            fours = full_count // 4

            def four(i, c):
                tile(slot, col, full_low + 4 * i, 4, span, False)
                return c

            lax.fori_loop(0, fours, four, 0)
            rest = full_count - 4 * fours
            start = full_low + 4 * fours

            def two(i, c):
                tile(slot, col, start, 2, span, False)
                return c

            lax.fori_loop(0, rest // 2, two, 0)

            def one(i, c):
                tile(slot, col, full_low + full_count - 1, 1, span, False)
                return c

            lax.fori_loop(0, rest % 2, one, 0)
            for half in range(2):
                for pair in range(2):
                    total = dq_acc[half, pair].T * SCALING
                    dq_ref[col, half, slot, 2 * pair : 2 * pair + 2] = total.reshape(2, ROWS, HEAD_DIM).astype(BF16)
            return carry

        lax.fori_loop(0, COLUMNS, column, 0)

    def finish(d, c):
        for slot in range(2):
            for half in range(2):
                rows = slice(half * ROWS, (half + 1) * ROWS)
                dkv_ref[d, half, slot, 0] = (dkv_acc[slot, 0, d, rows] * SCALING).astype(BF16)
                dkv_ref[d, half, slot, 1] = dkv_acc[slot, 1, d, rows].astype(BF16)
        return c

    lax.fori_loop(0, PLANES, finish, 0)


def grads(info, qd_all, kv_all, st_all):
    whole = pl.BlockSpec(memory_space=pltpu.VMEM)
    return pl.pallas_call(
        grads_kernel,
        in_specs=[pl.BlockSpec(memory_space=pltpu.SMEM), whole, whole, whole],
        out_specs=[whole, whole],
        out_shape=[
            jax.ShapeDtypeStruct((COLUMNS, 2, 2, GROUP, ROWS, HEAD_DIM), BF16),
            jax.ShapeDtypeStruct((PLANES, 2, 2, 2, ROWS, HEAD_DIM), BF16),
        ],
        scratch_shapes=[
            pltpu.VMEM((2, 2, HEAD_DIM, 256), F32),
            pltpu.VMEM((2, 2, PLANES, 256, HEAD_DIM), F32),
        ],
        compiler_params=pltpu.CompilerParams(vmem_limit_bytes=56 * 2**20),
        name="grads",
    )(info, qd_all, kv_all, st_all)


def collect_kernel(dq_ref, dkv_ref, rq, rkv, local, s_q, s_kv, r_q, r_kv):
    z, y, core = place()
    greet(z, y, core)
    other = 1 - core
    mine = [
        pltpu.make_async_copy(dq_ref.at[y, core], rq.at[y, core], local.at[0]),
        pltpu.make_async_copy(dkv_ref.at[0, core], rkv.at[0, core], local.at[1]),
    ]
    for c in mine:
        c.start()

    def query_send(dy, half):
        col = (y + dy) % 4
        return remote(dq_ref.at[col, half], rq.at[y, core], s_q.at[dy, half], r_q.at[y, core], at(z, col, half))

    def key_send(d, half, slot):
        return remote(
            dkv_ref.at[d, half, slot],
            rkv.at[d, core, slot],
            s_kv.at[d, half, slot],
            r_kv.at[d, core, slot],
            at((z + 8 - d) % 8, y, half),
        )

    def each_key_send(act):
        for d in range(PLANES - 1, 0, -1):
            for slot in range(2):
                if d <= max(FAR[0][slot], FAR[1][slot]):

                    @pl.when((z >= d) & (d <= far_of(core, slot)))
                    def _(d=d, slot=slot):
                        for half in range(2):
                            act(key_send(d, half, slot))

    sends = [query_send(dy, half) for dy in (2, 1, 3) for half in range(2)]
    sends.append(remote(dq_ref.at[y, other], rq.at[y, core], s_q.at[0, 0], r_q.at[y, core], at(z, y, other)))
    for slot in range(2):
        sends.append(
            remote(
                dkv_ref.at[0, other, slot],
                rkv.at[0, core, slot],
                s_kv.at[0, 0, slot],
                r_kv.at[0, core, slot],
                at(z, y, other),
            )
        )
    for c in sends:
        c.start()
    each_key_send(lambda c: c.start())

    to = at(z, y, other)

    def query_landed(col, c):
        return remote(dq_ref.at[0, 0], rq.at[col, c], s_q.at[0, 0], r_q.at[col, c], to)

    def key_landed(d, c, slot):
        return remote(dkv_ref.at[0, 0, slot], rkv.at[d, c, slot], s_kv.at[0, 0, slot], r_kv.at[d, c, slot], to)

    query_landed(y, other).wait_recv()
    for dy in range(1, COLUMNS):
        for c in range(2):
            query_landed((y + dy) % 4, c).wait_recv()
    for slot in range(2):
        key_landed(0, other, slot).wait_recv()
        for d in range(1, PLANES):
            for c in range(2):
                if d <= FAR[c][slot]:

                    @pl.when(z + d < PLANES)
                    def _(d=d, slot=slot, c=c):
                        key_landed(d, c, slot).wait_recv()

    for c in mine:
        c.wait()
    for c in sends:
        c.wait_send()
    each_key_send(lambda c: c.wait_send())


def collect(dq, dkv):
    anywhere = pl.BlockSpec(memory_space=pl.ANY)
    dma = pltpu.SemaphoreType.DMA
    return pl.pallas_call(
        collect_kernel,
        in_specs=[anywhere] * 2,
        out_specs=[anywhere] * 2,
        out_shape=[
            jax.ShapeDtypeStruct((COLUMNS, 2, 2, GROUP, ROWS, HEAD_DIM), BF16),
            jax.ShapeDtypeStruct((PLANES, 2, 2, 2, ROWS, HEAD_DIM), BF16),
        ],
        scratch_shapes=[
            dma((2,)),
            dma((COLUMNS, 2)),
            dma((PLANES, 2, 2)),
            dma((COLUMNS, 2)),
            dma((PLANES, 2, 2)),
        ],
        compiler_params=pltpu.CompilerParams(collective_id=1, has_side_effects=True),
        name="collect",
    )(dq, dkv)


def finish_kernel(info, rq_ref, rkv_ref, dq_ref, dk_ref, dv_ref):
    core, slot = pl.program_id(0), pl.program_id(1)
    for g in range(GROUP):
        total = rq_ref[0, 0, 0, g].astype(F32)
        for col in range(1, COLUMNS):
            total += rq_ref[col, 0, 0, g].astype(F32)
        dq_ref[:, g * HEAD_DIM : (g + 1) * HEAD_DIM] = total.astype(BF16)
    far = jnp.where(
        core == 0, jnp.where(slot == 0, FAR[0][0], FAR[0][1]), jnp.where(slot == 0, FAR[1][0], FAR[1][1])
    )
    last = jnp.minimum(far, PLANES - 1 - info[4])

    def add(d, carry):
        return carry[0] + rkv_ref[d, 0, 0, 0].astype(F32), carry[1] + rkv_ref[d, 0, 0, 1].astype(F32)

    dk, dv = lax.fori_loop(
        1, last + 1, add, (rkv_ref[0, 0, 0, 0].astype(F32), rkv_ref[0, 0, 0, 1].astype(F32))
    )
    dk_ref[...] = dk.astype(BF16)
    dv_ref[...] = dv.astype(BF16)


def finish(info, rq, rkv):
    return pl.pallas_call(
        finish_kernel,
        grid_spec=pltpu.PrefetchScalarGridSpec(
            num_scalar_prefetch=1,
            grid=(2, 2),
            in_specs=[
                pl.BlockSpec((COLUMNS, 1, 1, GROUP, ROWS, HEAD_DIM), lambda c, s, h: (0, c, s, 0, 0, 0)),
                pl.BlockSpec((PLANES, 1, 1, 2, ROWS, HEAD_DIM), lambda c, s, h: (0, c, s, 0, 0, 0)),
            ],
            out_specs=[
                pl.BlockSpec((ROWS, GROUP * HEAD_DIM), lambda c, s, h: (0, h[c * 2 + s])),
                pl.BlockSpec((ROWS, HEAD_DIM), lambda c, s, h: (0, h[c * 2 + s])),
                pl.BlockSpec((ROWS, HEAD_DIM), lambda c, s, h: (0, h[c * 2 + s])),
            ],
        ),
        out_shape=[
            jax.ShapeDtypeStruct((ROWS, Q_HEADS * HEAD_DIM), BF16),
            jax.ShapeDtypeStruct((ROWS, KV_HEADS * HEAD_DIM), BF16),
            jax.ShapeDtypeStruct((ROWS, KV_HEADS * HEAD_DIM), BF16),
        ],
        name="finish",
    )(info, rq, rkv)


def per_device(queries, keys, values, outputs, out_grad, log_sum_exp, spans):
    z, y, core = place()
    sequence = ROWS * lax.axis_size("ctx")
    numbers = jnp.arange(KV_HEADS, dtype=jnp.int32)

    def head_of(low, top):
        return jnp.sum(jnp.where((spans > low) & (spans <= top), numbers, 0))

    short = head_of(0, sequence // 16)
    middle = head_of(sequence // 8, sequence // 4)
    half = head_of(sequence // 4, sequence // 2)
    whole = head_of(sequence // 2, sequence)
    ordered = jnp.stack([whole, short, half, middle]).astype(jnp.int32)
    swapped = jnp.stack([half, middle, whole, short]).astype(jnp.int32)
    heads = jnp.where(core == 0, ordered, swapped)
    own_spans = jnp.stack(
        [jnp.sum(jnp.where(numbers == heads[slot], spans, 0)).astype(jnp.int32) for slot in range(2)]
    )
    info = jnp.concatenate([jnp.stack([z, y]).astype(jnp.int32), own_spans])
    qd, kv, st = pack(heads, queries, out_grad, outputs, keys, values, log_sum_exp)
    qd_all, kv_all, st_all = spread(qd, kv, st)
    dq, dkv = grads(info, qd_all, kv_all, st_all)
    rq, rkv = collect(dq, dkv)
    return tuple(finish(jnp.concatenate([ordered, jnp.stack([z]).astype(jnp.int32)]), rq, rkv))


def solution(mesh):
    in_specs = (
        P(("dp", "ctx"), None),
        P(("dp", "ctx"), None),
        P(("dp", "ctx"), None),
        P(("dp", "ctx"), None),
        P(("dp", "ctx"), None),
        P(None, ("dp", "ctx")),
        P("dp"),
    )
    out_specs = (P(("dp", "ctx"), None), P(("dp", "ctx"), None), P(("dp", "ctx"), None))
    return jax.shard_map(
        per_device, mesh=mesh, in_specs=in_specs, out_specs=out_specs, check_vma=False
    )
```

```python
import functools
import math

import jax
import jax.numpy as jnp
from jax import lax
from jax.experimental import pallas as pl
from jax.experimental.pallas import tpu as pltpu
from jax.sharding import PartitionSpec as P

Q_HEADS = 16
KV_HEADS = 4
GROUP = 4
HEAD_DIM = 128
PLANES = 8
COLUMNS = 4
ROWS = 128
SCALING = 1.0 / math.sqrt(HEAD_DIM)
LOG2E = math.log2(math.e)
BF16 = jnp.bfloat16
F32 = jnp.float32
MESH = pl.DeviceIdType.MESH
NT = (((1,), (1,)), ((), ()))
NN = (((1,), (0,)), ((), ()))
REACH = ((31, 2), (16, 8))
PLAIN = ((31, 0), (7, 3))
UP = ((3, 1), (4, 2))
DOWN = 4


def dot(a, b, dims=NN):
    return lax.dot_general(a, b, dims, preferred_element_type=F32)


def place():
    me = lax.axis_index("ctx")
    return me // 8, (me // 2) % 4, me % 2


def at(z, y, core):
    return {"ctx": z * 8 + y * 2 + core}


def remote(src, dst, send, recv, device):
    return pltpu.make_async_remote_copy(
        src_ref=src, dst_ref=dst, send_sem=send, recv_sem=recv, device_id=device, device_id_type=MESH
    )


def by_class(table, core, slot):
    first, second = table
    low = first[0] + (first[1] - first[0]) * slot
    high = second[0] + (second[1] - second[0]) * slot
    return low + (high - low) * core


def kernel(
    spans_ref,
    q_ref,
    k_ref,
    v_ref,
    o_ref,
    g_ref,
    lse_ref,
    dq_out,
    dk_out,
    dv_out,
    qd,
    kv,
    st,
    q_sib,
    kv_sib,
    st_sib,
    dq_acc,
    dkv_acc,
    dq_part,
    dq_in,
    dkv_send,
    dkv_in,
    fq,
    fkv,
    s_sib,
    r_sib,
    s_q,
    s_st,
    r_q,
    r_st,
    s_fq,
    s_fst,
    s_up,
    s_down,
    r_kv,
    s_dq,
    r_dq,
    s_dup,
    s_ddown,
    r_dkv,
    s_fin,
    r_fin,
):
    z, y, core = place()
    other = 1 - core
    sibling = at(z, y, other)
    before, after, across = (y + 3) % 4, (y + 1) % 4, (y + 2) % 4
    left, right, far = at(z, before, core), at(z, after, core), at(z, across, core)
    above, below = at((z + 1) % 8, y, core), at((z + 7) % 8, y, core)

    barrier = pltpu.get_barrier_semaphore()
    for peer in (sibling, left, right, far, above, below):
        pl.semaphore_signal(barrier, inc=1, device_id=peer, device_id_type=MESH)

    spans = [spans_ref[i] for i in range(KV_HEADS)]
    tops = ((4096, 8192), (0, 512), (2048, 4096), (1024, 2048))
    chosen_of, limits = [], []
    for low, top in tops:
        picks = [jnp.where((span > low) & (span <= top), 1, 0) for span in spans]
        chosen_of.append(picks)
        limits.append(sum(pick * span for pick, span in zip(picks, spans)))

    def pack(picks, q_to, kv_to, st_to):
        weights = [pick.astype(F32) for pick in picks]

        def taken(ref, g, width):
            total = None
            for head in range(KV_HEADS):
                first = head * width + g * HEAD_DIM
                term = ref[:, first : first + HEAD_DIM] * weights[head].astype(BF16)
                total = term if total is None else total + term
            return total

        st_to[...] = jnp.zeros((8, 256), F32)
        for g in range(GROUP):
            grad = taken(g_ref, g, 512)
            q_to[0, g] = taken(q_ref, g, 512)
            q_to[1, g] = grad
            product = grad.astype(F32) * taken(o_ref, g, 512).astype(F32)
            lanes = slice((g % 2) * ROWS, (g % 2 + 1) * ROWS)
            lse = sum(
                lse_ref[head * GROUP + g : head * GROUP + g + 1, :] * weights[head] for head in range(KV_HEADS)
            )
            st_to[g // 2 : g // 2 + 1, lanes] = lse * LOG2E
            st_to[2 + g // 2 : 3 + g // 2, lanes] = jnp.sum(product.T, axis=0, keepdims=True)
        kv_to[0] = taken(k_ref, 0, HEAD_DIM)
        kv_to[1] = taken(v_ref, 0, HEAD_DIM)

    for slot in range(2):
        theirs = [jnp.where(core == 0, a, b) for a, b in zip(chosen_of[2 + slot], chosen_of[slot])]
        pack(theirs, q_sib.at[slot], kv_sib.at[slot], st_sib.at[slot])

    pl.semaphore_wait(barrier, 6)

    sib_copies = [
        remote(kv_sib, kv.at[0, core], s_sib.at[0], r_sib.at[0], sibling),
        remote(q_sib, qd.at[y, core], s_sib.at[1], r_sib.at[1], sibling),
        remote(st_sib, st.at[y, core], s_sib.at[2], r_sib.at[2], sibling),
    ]
    for c in sib_copies:
        c.start()

    for slot in range(2):
        ours = [jnp.where(core == 0, a, b) for a, b in zip(chosen_of[slot], chosen_of[2 + slot])]
        pack(ours, qd.at[y, core, slot], kv.at[0, core, slot], st.at[y, core, slot])

    def q_copy(half, slot, way):
        return remote(
            qd.at[y, half, slot],
            qd.at[y, half, slot],
            s_q.at[half, slot, way],
            r_q.at[y, half, slot],
            right if way == 0 else left,
        )

    def st_copy(half, way):
        return remote(
            st.at[y, half], st.at[y, half], s_st.at[half, way], r_st.at[y, half], right if way == 0 else left
        )

    def start_q(half):
        for way in range(2):
            st_copy(half, way).start()
        for way in range(2):
            q_copy(half, way, way).start()
        for way in range(2):
            q_copy(half, 1 - way, way).start()

    start_q(core)

    def up_copy(d, slot):
        return remote(kv.at[d, :, slot], kv.at[d + 1, :, slot], s_up.at[d, slot], r_kv.at[d + 1, slot], above)

    def down_copy(e):
        return remote(
            kv.at[(8 - e) % 8, :, 0], kv.at[7 - e, :, 0], s_down.at[e], r_kv.at[7 - e, 0], below
        )

    def goes_up(d, slot):
        return (z + 1 < PLANES) & (z >= d) & (d < by_class(UP, core, slot))

    def goes_down(e):
        return (core == 0) & (e < DOWN) & ((z + e) % 8 < DOWN)

    def forward(i):
        for slot in range(2):

            @pl.when(goes_up(i, slot))
            def _(slot=slot):
                up_copy(i, slot).start()

        @pl.when(goes_down(i))
        def _():
            down_copy(i).start()

    def kv_landed(d, slot):
        return remote(kv.at[0, :, 0], kv.at[d, :, slot], s_up.at[0, 0], r_kv.at[d, slot], sibling)

    def arrive(i):
        for slot in range(2):

            @pl.when((z >= i) & (i <= by_class(UP, core, slot)))
            def _(slot=slot):
                kv_landed(i, slot).wait_recv()

        @pl.when((core == 0) & ((z + i) % 8 < DOWN))
        def _():
            kv_landed(8 - i, 0).wait_recv()

    sib_copies[0].wait_recv()
    forward(0)
    sib_copies[1].wait_recv()
    sib_copies[2].wait_recv()
    start_q(other)

    dkv_acc[...] = jnp.zeros_like(dkv_acc)
    own_limits = [jnp.where(core == 0, limits[slot], limits[2 + slot]) for slot in range(2)]

    def tile(slot, col, d0, count, masked):
        size = count * 256
        k = kv[pl.ds(d0, count), :, slot, 0].reshape(size, HEAD_DIM)
        v = kv[pl.ds(d0, count), :, slot, 1].reshape(size, HEAD_DIM)
        k_t = k.T
        for half in range(2):
            for pair in range(2):
                chosen = slice(2 * pair, 2 * pair + 2)
                q = qd[col, half, slot, 0, chosen].reshape(256, HEAD_DIM)
                g = qd[col, half, slot, 1, chosen].reshape(256, HEAD_DIM)
                lse = st[col, half, slot, pair : pair + 1]
                delta = st[col, half, slot, 2 + pair : 3 + pair]
                prob = jnp.exp2(dot(k, q, NT) * (SCALING * LOG2E) - lse)
                if masked:
                    limit = jnp.where(slot == 0, own_limits[0], own_limits[1])
                    key = lax.broadcasted_iota(jnp.int32, (size, 256), 0)
                    row = lax.broadcasted_iota(jnp.int32, (size, 256), 1) % ROWS
                    distance = row - key + (d0 * 1024 + (col - y) * 256 + half * ROWS)
                    prob = jnp.where((distance >= 0) & (distance < limit), prob, 0.0)
                ds = (prob * (dot(v, g, NT) - delta)).astype(BF16)
                low = prob.astype(BF16)
                dkv_acc[slot, 0, pl.ds(d0, count)] += dot(ds, q).reshape(count, 256, HEAD_DIM)
                dkv_acc[slot, 1, pl.ds(d0, count)] += dot(low, g).reshape(count, 256, HEAD_DIM)
                dq_acc[slot, half, pair] += dot(k_t, ds)

    def last_block(table, slot, ahead):
        return jnp.minimum(z, (by_class(table, core, slot) - ahead + 4) // 4 - 1)

    def write_dq(col, slot):
        for half in range(2):
            for pair in range(2):
                total = dq_acc[slot, half, pair].T * SCALING
                dq_part[col, slot, half, 2 * pair : 2 * pair + 2] = total.reshape(2, ROWS, HEAD_DIM).astype(BF16)

    dq_acc[...] = jnp.zeros_like(dq_acc)

    def diagonal(slot, carry):
        tile(slot, y, 0, 1, True)
        return carry

    lax.fori_loop(0, 2, diagonal, 0)

    def step(i, carry):
        arrive(i)
        forward(i)

        def one_slot(slot, c):
            full, end = last_block(PLAIN, slot, 0), last_block(REACH, slot, 0)
            here = (i <= by_class(UP, core, slot)) & (i <= end)

            @pl.when(here & (i <= full))
            def _():
                tile(slot, y, i, 1, False)

            @pl.when(here & (i > full))
            def _():
                tile(slot, y, i, 1, True)

            return c

        lax.fori_loop(0, 2, one_slot, 0)

        @pl.when((core == 0) & (z >= 8 - i))
        def _():
            tile(0, y, 8 - i, 1, False)

        return carry

    lax.fori_loop(1, 5, step, 0)
    for slot in range(2):
        write_dq(y, slot)

    def q_landed(col, half, slot):
        return remote(qd.at[0, 0, 0], qd.at[col, half, slot], s_q.at[0, 0, 0], r_q.at[col, half, slot], sibling)

    def st_landed(col, half):
        return remote(st.at[0, 0], st.at[col, half], s_st.at[0, 0], r_st.at[col, half], sibling)

    forwards = []
    for half in range(2):
        st_landed(before, half).wait_recv()
        forwards.append(remote(st.at[before, half], st.at[before, half], s_fst.at[half], r_st.at[before, half], right))
        forwards[-1].start()
        q_landed(before, half, 0).wait_recv()
        forwards.append(
            remote(qd.at[before, half, 0], qd.at[before, half, 0], s_fq.at[half, 0], r_q.at[before, half, 0], right)
        )
        forwards[-1].start()
        q_landed(after, half, 1).wait_recv()
        forwards.append(
            remote(qd.at[after, half, 1], qd.at[after, half, 1], s_fq.at[half, 1], r_q.at[after, half, 1], left)
        )
        forwards[-1].start()

    def dq_copy(dy, slot):
        col = (y + dy) % 4
        return remote(
            dq_part.at[col, slot], dq_in.at[y, slot], s_dq.at[dy, slot], r_dq.at[y, slot], at(z, col, core)
        )

    def one_column(n, carry):
        dy = n + (n // 2) * (1 - 2 * (n % 2))
        col = (y + dy) % 4
        ahead = col - y
        dq_acc[...] = jnp.zeros_like(dq_acc)
        for half in range(2):

            @pl.when(dy != 3)
            def _(half=half):
                st_landed(col, half).wait_recv()

            @pl.when(dy != 3)
            def _(half=half):
                q_landed(col, half, 0).wait_recv()

            @pl.when(dy != 1)
            def _(half=half):
                q_landed(col, half, 1).wait_recv()

        def one_slot(slot, c):
            first = jnp.where(ahead > 0, 0, 1)
            full, end = last_block(PLAIN, slot, ahead), last_block(REACH, slot, ahead)
            large = (core == 0) & (slot == 0) & (z >= 3)
            below_count = jnp.where(large, 1 - first, jnp.maximum(full - first + 1, 0))
            above_count = jnp.where(large & (z < 7), z - 3, 0)

            def plain(m, cc):
                d = jnp.where(m < below_count, first + m, 4 + m - below_count)
                tile(slot, col, d, 1, False)
                return cc

            lax.fori_loop(0, below_count + above_count, plain, 0)

            def masked(d, cc):
                tile(slot, col, d, 1, True)
                return cc

            lax.fori_loop(jnp.maximum(full + 1, first), end + 1, masked, 0)

            @pl.when(large)
            def _():
                tile(0, col, 1, 3, False)

            @pl.when(large & (z == 7))
            def _():
                tile(0, col, 4, 4, False)

            write_dq(col, slot)
            dq_copy(dy, slot).start()
            return c

        lax.fori_loop(0, 2, one_slot, 0)
        return carry

    lax.fori_loop(1, COLUMNS, one_column, 0)

    def dkv_down(d, slot):
        return remote(
            dkv_send.at[slot, d], dkv_in.at[slot, d - 1], s_ddown.at[slot, d], r_dkv.at[slot, d - 1], below
        )

    def dkv_up(e):
        return remote(dkv_send.at[0, 8 - e], dkv_in.at[0, 9 - e], s_dup.at[e], r_dkv.at[0, 9 - e], above)

    def dkv_landed(slot, d):
        return remote(dkv_send.at[0, 0], dkv_in.at[slot, d], s_dup.at[0], r_dkv.at[slot, d], sibling)

    scales = (SCALING, 1.0)

    def returns_down(i, slot):
        return (z >= i) & (i <= by_class(UP, core, slot))

    def returns_up(i):
        return (core == 0) & ((z + i) % 8 < DOWN)

    def back(n, carry):
        i = 4 - n
        for slot in range(2):
            joined = (z + 1 < PLANES) & (i < by_class(UP, core, slot))

            @pl.when(returns_down(i, slot) & joined)
            def _(slot=slot):
                dkv_landed(slot, i).wait_recv()
                for part in range(2):
                    total = dkv_acc[slot, part, i] * scales[part] + dkv_in[slot, i, part].astype(F32)
                    dkv_send[slot, i, part] = total.astype(BF16)

            @pl.when(returns_down(i, slot) & jnp.logical_not(joined))
            def _(slot=slot):
                for part in range(2):
                    dkv_send[slot, i, part] = (dkv_acc[slot, part, i] * scales[part]).astype(BF16)

            @pl.when(returns_down(i, slot))
            def _(slot=slot):
                dkv_down(i, slot).start()

        @pl.when(returns_up(i) & (i < DOWN))
        def _():
            dkv_landed(0, 8 - i).wait_recv()
            for part in range(2):
                total = dkv_acc[0, part, 8 - i] * scales[part] + dkv_in[0, 8 - i, part].astype(F32)
                dkv_send[0, 8 - i, part] = total.astype(BF16)

        @pl.when(returns_up(i) & (i == DOWN))
        def _():
            for part in range(2):
                dkv_send[0, 4, part] = (dkv_acc[0, part, 4] * scales[part]).astype(BF16)

        @pl.when(returns_up(i))
        def _():
            dkv_up(i).start()

        return carry

    lax.fori_loop(0, 4, back, 0)

    for slot in range(2):
        for dy in range(1, COLUMNS):
            col = (y + dy) % 4
            remote(dq_part.at[0, 0], dq_in.at[col, slot], s_dq.at[0, 0], r_dq.at[col, slot], sibling).wait_recv()
        for part_half in range(2):
            half = core if part_half == 1 else other
            for g in range(GROUP):
                total = dq_part[y, slot, half, g].astype(F32)
                for dy in range(1, COLUMNS):
                    total += dq_in[(y + dy) % 4, slot, half, g].astype(F32)
                fq[part_half, slot, g] = total.astype(BF16)
    q_fin = remote(fq.at[0], fq.at[2], s_fin.at[0], r_fin.at[0], sibling)
    q_fin.start()

    @pl.when(z + 1 < PLANES)
    def _():
        for slot in range(2):
            dkv_landed(slot, 0).wait_recv()
            for part in range(2):
                dkv_acc[slot, part, 0] = dkv_acc[slot, part, 0] * scales[part] + dkv_in[slot, 0, part].astype(F32)

    @pl.when(z + 1 == PLANES)
    def _():
        for slot in range(2):
            dkv_acc[slot, 0, 0] = dkv_acc[slot, 0, 0] * SCALING

    @pl.when((core == 0) & (z < DOWN))
    def _():
        dkv_landed(0, 8).wait_recv()
        for part in range(2):
            dkv_acc[0, part, 0] = dkv_acc[0, part, 0] + dkv_in[0, 8, part].astype(F32)

    for slot in range(2):
        for part in range(2):
            for part_half in range(2):
                half = core if part_half == 1 else other
                rows = pl.ds(pl.multiple_of(half * ROWS, ROWS), ROWS)
                fkv[part_half, slot, part] = dkv_acc[slot, part, 0, rows].astype(BF16)
    kv_fin = remote(fkv.at[0], fkv.at[2], s_fin.at[1], r_fin.at[1], sibling)
    kv_fin.start()
    q_fin.wait_recv()
    kv_fin.wait_recv()

    def entry(kind):
        return 1 + (core + kind // 2) % 2

    for head in range(KV_HEADS):
        masks = [jnp.full((ROWS, HEAD_DIM), chosen_of[kind][head], jnp.int32) > 0 for kind in range(4)]

        def picked(read):
            total = jnp.zeros((ROWS, HEAD_DIM), F32)
            for kind in range(4):
                total = jnp.where(masks[kind], read(entry(kind), kind % 2).astype(F32), total)
            return total.astype(BF16)

        for g in range(GROUP):
            cols = slice((head * GROUP + g) * HEAD_DIM, (head * GROUP + g + 1) * HEAD_DIM)
            dq_out[:, cols] = picked(lambda e, slot, g=g: fq[e, slot, g])
        cols = slice(head * HEAD_DIM, (head + 1) * HEAD_DIM)
        dk_out[:, cols] = picked(lambda e, slot: fkv[e, slot, 0])
        dv_out[:, cols] = picked(lambda e, slot: fkv[e, slot, 1])

    for c in sib_copies + forwards + [q_fin, kv_fin]:
        c.wait_send()
    for half in range(2):
        for way in range(2):
            st_copy(half, way).wait_send()
            for slot in range(2):
                q_copy(half, slot, way).wait_send()
    for dy in range(1, COLUMNS):
        for slot in range(2):
            dq_copy(dy, slot).wait_send()

    def sent(i, carry):
        for slot in range(2):

            @pl.when(goes_up(i, slot))
            def _(slot=slot):
                up_copy(i, slot).wait_send()

            @pl.when((i > 0) & returns_down(i, slot))
            def _(slot=slot):
                dkv_down(i, slot).wait_send()

        @pl.when(goes_down(i))
        def _():
            down_copy(i).wait_send()

        @pl.when((i > 0) & returns_up(i))
        def _():
            dkv_up(i).wait_send()

        return carry

    lax.fori_loop(0, 5, sent, 0)


def per_device(queries, keys, values, outputs, out_grad, log_sum_exp, spans):
    whole = pl.BlockSpec(memory_space=pltpu.VMEM)
    dma = pltpu.SemaphoreType.DMA
    return tuple(
        pl.pallas_call(
            kernel,
            in_specs=[pl.BlockSpec(memory_space=pltpu.SMEM)] + [whole] * 6,
            out_specs=[whole] * 3,
            out_shape=[
                jax.ShapeDtypeStruct((ROWS, Q_HEADS * HEAD_DIM), BF16),
                jax.ShapeDtypeStruct((ROWS, KV_HEADS * HEAD_DIM), BF16),
                jax.ShapeDtypeStruct((ROWS, KV_HEADS * HEAD_DIM), BF16),
            ],
            scratch_shapes=[
                pltpu.VMEM((COLUMNS, 2, 2, 2, GROUP, ROWS, HEAD_DIM), BF16),
                pltpu.VMEM((PLANES, 2, 2, 2, ROWS, HEAD_DIM), BF16),
                pltpu.VMEM((COLUMNS, 2, 2, 8, 256), F32),
                pltpu.VMEM((2, 2, GROUP, ROWS, HEAD_DIM), BF16),
                pltpu.VMEM((2, 2, ROWS, HEAD_DIM), BF16),
                pltpu.VMEM((2, 8, 256), F32),
                pltpu.VMEM((2, 2, 2, HEAD_DIM, 256), F32),
                pltpu.VMEM((2, 2, PLANES, 256, HEAD_DIM), F32),
                pltpu.VMEM((COLUMNS, 2, 2, GROUP, ROWS, HEAD_DIM), BF16),
                pltpu.VMEM((COLUMNS, 2, 2, GROUP, ROWS, HEAD_DIM), BF16),
                pltpu.VMEM((2, PLANES, 2, 256, HEAD_DIM), BF16),
                pltpu.VMEM((2, PLANES + 1, 2, 256, HEAD_DIM), BF16),
                pltpu.VMEM((3, 2, GROUP, ROWS, HEAD_DIM), BF16),
                pltpu.VMEM((3, 2, 2, ROWS, HEAD_DIM), BF16),
                dma((3,)),
                dma((3,)),
                dma((2, 2, 2)),
                dma((2, 2)),
                dma((COLUMNS, 2, 2)),
                dma((COLUMNS, 2)),
                dma((2, 2)),
                dma((2,)),
                dma((PLANES, 2)),
                dma((PLANES,)),
                dma((PLANES, 2)),
                dma((COLUMNS, 2)),
                dma((COLUMNS, 2)),
                dma((PLANES,)),
                dma((2, PLANES)),
                dma((2, PLANES + 1)),
                dma((2,)),
                dma((2,)),
            ],
            compiler_params=pltpu.CompilerParams(
                collective_id=0, has_side_effects=True, vmem_limit_bytes=56 * 2**20
            ),
            name="gradients",
        )(spans, queries, keys, values, outputs, out_grad, log_sum_exp)
    )


def solution(mesh):
    in_specs = (
        P(("dp", "ctx"), None),
        P(("dp", "ctx"), None),
        P(("dp", "ctx"), None),
        P(("dp", "ctx"), None),
        P(("dp", "ctx"), None),
        P(None, ("dp", "ctx")),
        P("dp"),
    )
    out_specs = (P(("dp", "ctx"), None), P(("dp", "ctx"), None), P(("dp", "ctx"), None))
    return jax.shard_map(
        per_device, mesh=mesh, in_specs=in_specs, out_specs=out_specs, check_vma=False
    )
```

```python
import functools
import math

import jax
import jax.numpy as jnp
from jax import lax
from jax.experimental import pallas as pl
from jax.experimental.pallas import tpu as pltpu
from jax.sharding import PartitionSpec as P

Q_HEADS = 16
KV_HEADS = 4
GROUP = 4
HEAD_DIM = 128
PLANES = 8
COLUMNS = 4
ROWS = 128
SCALING = 1.0 / math.sqrt(HEAD_DIM)
LOG2E = math.log2(math.e)
BF16 = jnp.bfloat16
F32 = jnp.float32
MESH = pl.DeviceIdType.MESH
NT = (((1,), (1,)), ((), ()))
NN = (((1,), (0,)), ((), ()))
CHIPS = PLANES * COLUMNS
REACH = ((31, 2), (16, 8))
PLAIN = ((31, 0), (7, 3))
UP = (3, 4)
DOWN = 4
NEAR = 2


def dot(a, b, dims=NN):
    return lax.dot_general(a, b, dims, preferred_element_type=F32)


def place():
    me = lax.axis_index("ctx")
    return me // 8, (me // 2) % 4, me % 2


def at(z, y, core):
    return {"ctx": z * 8 + y * 2 + core}


def remote(src, dst, send, recv, device):
    return pltpu.make_async_remote_copy(
        src_ref=src, dst_ref=dst, send_sem=send, recv_sem=recv, device_id=device, device_id_type=MESH
    )


def by_class(table, core, slot):
    first, second = table
    low = first[0] + (first[1] - first[0]) * slot
    high = second[0] + (second[1] - second[0]) * slot
    return low + (high - low) * core


def kernel(
    spans_ref,
    q_ref,
    k_ref,
    v_ref,
    o_ref,
    g_ref,
    lse_ref,
    dq_out,
    dk_out,
    dv_out,
    qd,
    kv,
    kv1,
    st,
    q_sib,
    kv_sib,
    st_sib,
    dq_acc,
    dkv_acc,
    dkv1_acc,
    dq_part,
    dq_in,
    dkv_send,
    dkv_in,
    near_send,
    near_in,
    fq,
    fkv,
    s_sib,
    r_sib,
    s_q,
    s_st,
    r_q,
    r_st,
    s_fq,
    s_fst,
    s_up,
    s_down,
    r_kv,
    s_near,
    r_near,
    s_dq,
    r_dq,
    s_dkv,
    r_dkv,
    s_nback,
    r_nback,
    s_fin,
    r_fin,
):
    z, y, core = place()
    other = 1 - core
    up_reach = UP[0] + (UP[1] - UP[0]) * core
    chip = z * COLUMNS + y
    home = y * core
    sibling = at(z, y, other)
    before, after, across = (y + 3) % 4, (y + 1) % 4, (y + 2) % 4
    left, right, far = at(z, before, core), at(z, after, core), at(z, across, core)
    above, below = at((z + 1) % 8, y, core), at((z + 7) % 8, y, core)

    def at_chip(number):
        return at(number // COLUMNS, number % COLUMNS, core)

    def feeds(j):
        return (core == 0) & (chip + j < CHIPS)

    def fed_by(j):
        return (core == 0) & (chip >= j)

    barrier = pltpu.get_barrier_semaphore()
    for peer in (sibling, left, right, far):
        pl.semaphore_signal(barrier, inc=1, device_id=peer, device_id_type=MESH)
    for dz in range(1, PLANES):
        pl.semaphore_signal(barrier, inc=1, device_id=at((z + dz) % 8, y, core), device_id_type=MESH)
    for j in range(1, NEAR + 1):

        @pl.when(feeds(j))
        def _(j=j):
            pl.semaphore_signal(barrier, inc=1, device_id=at_chip(chip + j), device_id_type=MESH)

        @pl.when(fed_by(j))
        def _(j=j):
            pl.semaphore_signal(barrier, inc=1, device_id=at_chip(chip - j), device_id_type=MESH)

    greetings = 11 + (1 - core) * (jnp.minimum(NEAR, chip) + jnp.minimum(NEAR, CHIPS - 1 - chip))

    spans = [spans_ref[i] for i in range(KV_HEADS)]
    tops = ((4096, 8192), (0, 512), (2048, 4096), (1024, 2048))
    chosen_of, limits = [], []
    for low, top in tops:
        picks = [jnp.where((span > low) & (span <= top), 1, 0) for span in spans]
        chosen_of.append(picks)
        limits.append(sum(pick * span for pick, span in zip(picks, spans)))

    def taker(picks):
        weights = [pick.astype(F32) for pick in picks]

        def taken(ref, g, width):
            total = None
            for head in range(KV_HEADS):
                first = head * width + g * HEAD_DIM
                term = ref[:, first : first + HEAD_DIM] * weights[head].astype(BF16)
                total = term if total is None else total + term
            return total

        return weights, taken

    def pack_queries(picks, q_to, st_to):
        weights, taken = taker(picks)
        st_to[...] = jnp.zeros((8, 256), F32)
        for g in range(GROUP):
            grad = taken(g_ref, g, 512)
            q_to[0, g] = taken(q_ref, g, 512)
            q_to[1, g] = grad
            product = grad.astype(F32) * taken(o_ref, g, 512).astype(F32)
            lanes = slice((g % 2) * ROWS, (g % 2 + 1) * ROWS)
            lse = sum(
                lse_ref[head * GROUP + g : head * GROUP + g + 1, :] * weights[head] for head in range(KV_HEADS)
            )
            st_to[g // 2 : g // 2 + 1, lanes] = lse * LOG2E
            st_to[2 + g // 2 : 3 + g // 2, lanes] = jnp.sum(product.T, axis=0, keepdims=True)

    def pack_keys(picks, kv_to):
        taken = taker(picks)[1]
        kv_to[0] = taken(k_ref, 0, HEAD_DIM)
        kv_to[1] = taken(v_ref, 0, HEAD_DIM)

    theirs = [
        [jnp.where(core == 0, a, b) for a, b in zip(chosen_of[2 + slot], chosen_of[slot])] for slot in range(2)
    ]
    ours = [[jnp.where(core == 0, a, b) for a, b in zip(chosen_of[slot], chosen_of[2 + slot])] for slot in range(2)]

    def q_copy(half, slot, way):
        return remote(
            qd.at[y, half, slot],
            qd.at[y, half, slot],
            s_q.at[half, slot, way],
            r_q.at[y, half, slot],
            right if way == 0 else left,
        )

    def st_copy(half, slot, way):
        return remote(
            st.at[y, half, slot],
            st.at[y, half, slot],
            s_st.at[half, slot, way],
            r_st.at[y, half, slot],
            right if way == 0 else left,
        )

    def start_q(half, slot):
        for way in range(2):
            st_copy(half, slot, way).start()
            q_copy(half, slot, way).start()

    sib_copies = [
        remote(kv_sib.at[0], kv.at[0, core], s_sib.at[4], r_sib.at[4], sibling),
    ]
    for slot in range(2):
        sib_copies.append(remote(q_sib.at[slot], qd.at[y, core, slot], s_sib.at[slot], r_sib.at[slot], sibling))
        sib_copies.append(
            remote(st_sib.at[slot], st.at[y, core, slot], s_sib.at[2 + slot], r_sib.at[2 + slot], sibling)
        )

    sib_copies.append(remote(kv_sib.at[1], kv1.at[y * other, core], s_sib.at[5], r_sib.at[5], sibling))

    for slot in range(2):
        pack_keys(theirs[slot], kv_sib.at[slot])
    pl.semaphore_wait(barrier, greetings)
    sib_copies[0].start()
    sib_copies[5].start()
    pack_keys(ours[0], kv.at[0, core])
    pack_keys(ours[1], kv1.at[home, core])
    pack_queries(theirs[0], q_sib.at[0], st_sib.at[0])
    sib_copies[1].start()
    sib_copies[2].start()
    pack_queries(ours[0], qd.at[y, core, 0], st.at[y, core, 0])
    start_q(core, 0)

    def up_copy(d, part):
        return remote(
            kv.at[d, :, part], kv.at[d + 1, :, part], s_up.at[d, part], r_kv.at[d + 1, part], above
        )

    def down_copy(e, part):
        return remote(
            kv.at[(8 - e) % 8, :, part], kv.at[7 - e, :, part], s_down.at[e, part], r_kv.at[7 - e, part], below
        )

    def goes_up(d):
        return (z + 1 < PLANES) & (z >= d) & (d < up_reach)

    def goes_down(e):
        return (core == 0) & (e < DOWN) & ((z + e) % 8 < DOWN)

    def kv_landed(d, part):
        return remote(kv.at[0, :, 0], kv.at[d, :, part], s_up.at[0, 0], r_kv.at[d, part], sibling)

    def hop(i):
        for part in range(2):
            if not isinstance(i, int):

                @pl.when((z >= i) & (i <= up_reach))
                def _(part=part):
                    kv_landed(i, part).wait_recv()

            @pl.when(goes_up(i))
            def _(part=part):
                up_copy(i, part).start()

            if not isinstance(i, int):

                @pl.when((core == 0) & ((z + i) % 8 < DOWN))
                def _(part=part):
                    kv_landed(8 - i, part).wait_recv()

            @pl.when(goes_down(i))
            def _(part=part):
                down_copy(i, part).start()

    def near_copy(j):
        return remote(kv1.at[0], kv1.at[j], s_near.at[j], r_near.at[j], at_chip(chip + j))

    def lift_copy(d):
        return remote(kv1.at[4 * d + y], kv1.at[4 * d + 4 + y], s_near.at[d], r_near.at[4 * d + 4 + y], above)

    def round_copy(d, dy):
        block = 4 * d + y
        return remote(kv1.at[block], kv1.at[block], s_near.at[3 * d + dy + 2], r_near.at[block], at(z, (y + dy) % 4, core))

    def near_landed(block):
        return remote(kv1.at[0], kv1.at[block], s_near.at[0], r_near.at[block], sibling)

    def lifts(d):
        return (core == 1) & (d < 2) & (z >= d) & (z + 1 < PLANES)

    def rounds(d, dy):
        col = (y + dy) % 4
        blocks = 4 * d + col - y
        return (core == 1) & (z >= d) & (blocks >= 0) & (blocks <= REACH[1][1])

    def lift(d):
        if d > 0:

            @pl.when((core == 1) & (z >= d))
            def _():
                near_landed(4 * d + y).wait_recv()

        if d < 2:

            @pl.when(lifts(d))
            def _():
                lift_copy(d).start()

        for dy in (1, 3, 2):

            @pl.when(rounds(d, dy))
            def _(dy=dy):
                round_copy(d, dy).start()

    def start_near():
        for j in range(1, NEAR + 1):

            @pl.when(feeds(j))
            def _(j=j):
                near_copy(j).start()

        lift(0)

    sib_copies[0].wait_recv()
    hop(0)
    sib_copies[5].wait_recv()
    start_near()
    pack_queries(theirs[1], q_sib.at[1], st_sib.at[1])
    sib_copies[3].start()
    sib_copies[4].start()
    sib_copies[1].wait_recv()
    sib_copies[2].wait_recv()
    start_q(other, 0)
    pack_queries(ours[1], qd.at[y, core, 1], st.at[y, core, 1])

    dkv_acc[...] = jnp.zeros_like(dkv_acc)
    dkv1_acc[...] = jnp.zeros_like(dkv1_acc)
    own_limits = [jnp.where(core == 0, limits[slot], limits[2 + slot]) for slot in range(2)]

    def tile(slot, col, d0, count, masked, blocks=0):
        size = count * 256
        keys, acc = (kv, dkv_acc) if slot == 0 else (kv1, dkv1_acc)
        into = pl.ds(d0, count)
        k = keys[pl.ds(d0, count), :, 0].reshape(size, HEAD_DIM)
        v = keys[pl.ds(d0, count), :, 1].reshape(size, HEAD_DIM)
        k_t = k.T
        base = d0 * 1024 + (col - y) * 256 if slot == 0 else blocks * 256
        if count == 1:
            groups = [[(half, pair) for half in range(2) for pair in range(2)]]
        else:
            groups = [[(half, pair)] for half in range(2) for pair in range(2)]
        for group in groups:
            width = 256 * len(group)

            def rows(what, group=group, width=width):
                return jnp.concatenate(
                    [
                        qd[col, half, slot, what, 2 * pair : 2 * pair + 2].reshape(256, HEAD_DIM)
                        for half, pair in group
                    ],
                    axis=0,
                )

            def stats(first, group=group):
                return jnp.concatenate(
                    [st[col, half, slot, first + pair : first + pair + 1] for half, pair in group], axis=1
                )

            q, g = rows(0), rows(1)
            prob = jnp.exp2(dot(k, q, NT) * (SCALING * LOG2E) - stats(0))
            if masked:
                key = lax.broadcasted_iota(jnp.int32, (size, width), 0)
                lane = lax.broadcasted_iota(jnp.int32, (size, width), 1)
                row = lane % ROWS + lane // 512 * ROWS
                distance = row - key + base
                prob = jnp.where((distance >= 0) & (distance < own_limits[slot]), prob, 0.0)
            ds = (prob * (dot(v, g, NT) - stats(2))).astype(BF16)
            low = prob.astype(BF16)
            acc[0, into] += dot(ds, q).reshape(count, 256, HEAD_DIM)
            acc[1, into] += dot(low, g).reshape(count, 256, HEAD_DIM)
            change = dot(k_t, ds)
            for n, (half, pair) in enumerate(group):
                dq_acc[slot, half, pair] += change[:, n * 256 : (n + 1) * 256]

    def last_block(table, slot, ahead):
        return jnp.minimum(z, (by_class(table, core, slot) - ahead + 4) // 4 - 1)

    def write_dq(col, slot):
        for half in range(2):
            for pair in range(2):
                total = dq_acc[slot, half, pair].T * SCALING
                dq_part[col, slot, half, 2 * pair : 2 * pair + 2] = total.reshape(2, ROWS, HEAD_DIM).astype(BF16)

    def q_landed(col, half, slot):
        return remote(qd.at[0, 0, 0], qd.at[col, half, slot], s_q.at[0, 0, 0], r_q.at[col, half, slot], sibling)

    def st_landed(col, half, slot):
        return remote(st.at[0, 0, 0], st.at[col, half, slot], s_st.at[0, 0, 0], r_st.at[col, half, slot], sibling)

    def q_forward(slot, half):
        col, to = (before, right) if half == 0 else (after, left)
        return (
            remote(
                st.at[col, half, slot], st.at[col, half, slot], s_fst.at[slot, half], r_st.at[col, half, slot], to
            ),
            remote(qd.at[col, half, slot], qd.at[col, half, slot], s_fq.at[slot, half], r_q.at[col, half, slot], to),
        )

    def pass_queries(slot):
        for half in range(2):
            col = before if half == 0 else after
            st_landed(col, half, slot).wait_recv()
            q_landed(col, half, slot).wait_recv()
            for c in q_forward(slot, half):
                c.start()

    def await_queries(slot, dy):
        col = (y + dy) % 4
        for half in range(2):

            @pl.when((dy != 3) if half == 0 else (dy != 1))
            def _(half=half):
                st_landed(col, half, slot).wait_recv()
                q_landed(col, half, slot).wait_recv()

    dq_acc[...] = jnp.zeros_like(dq_acc)
    tile(0, y, 0, 1, True)

    def step(i, carry):
        @pl.when(i == 4)
        def _():
            pass_queries(0)

        hop(i)

        @pl.when(i == 3)
        def _():
            lift(1)

        @pl.when(i == 4)
        def _():
            lift(2)

        full, end = last_block(PLAIN, 0, 0), last_block(REACH, 0, 0)
        here = (i <= up_reach) & (i <= end)

        @pl.when(here & (i <= full))
        def _():
            tile(0, y, i, 1, False)

        @pl.when(here & (i > full))
        def _():
            tile(0, y, i, 1, True)

        @pl.when((core == 0) & (z >= 8 - i))
        def _():
            tile(0, y, 8 - i, 1, False)

        return carry

    lax.fori_loop(1, 5, step, 0)
    write_dq(y, 0)
    sib_copies[3].wait_recv()
    sib_copies[4].wait_recv()

    def dq_copy(dy):
        col = (y + dy) % 4
        return remote(dq_part.at[col, 0], dq_in.at[y], s_dq.at[dy], r_dq.at[y], at(z, col, core))

    scales = (SCALING, 1.0)

    def dkv_landed(d):
        return remote(dkv_send.at[0], dkv_in.at[d], s_dkv.at[0], r_dkv.at[d], sibling)

    def dkv_back(d):
        return remote(dkv_send.at[d], dkv_in.at[d], s_dkv.at[d], r_dkv.at[d], at((z + 8 - d) % 8, y, core))

    def dkv_join(d):
        return remote(dkv_send.at[d], dkv_in.at[d], s_dkv.at[d], r_dkv.at[d], at((z + 10 - d) % 8, y, core))

    def ready(d):
        for part in range(2):
            dkv_send[d, part] = (dkv_acc[part, d] * scales[part]).astype(BF16)

    def start_back(d):
        ready(d)
        dkv_back(d).start()

    def first_level():
        @pl.when((core == 1) & (z >= 4))
        def _():
            ready(4)
            dkv_join(4).start()

        @pl.when(z >= 3)
        def _():
            ready(3)
            dkv_join(3).start()

        @pl.when(z >= 1)
        def _():
            start_back(1)

    def second_level():
        @pl.when(z >= 2)
        def _():
            for part in range(2):
                dkv_acc[part, 2] = dkv_acc[part, 2] * scales[part]

            for d in (3, 4):

                @pl.when((z + d - 2 < PLANES) & (core >= d - 3))
                def _(d=d):
                    dkv_landed(d).wait_recv()
                    for part in range(2):
                        dkv_acc[part, 2] = dkv_acc[part, 2] + dkv_in[d, part].astype(F32)

            for part in range(2):
                dkv_send[2, part] = dkv_acc[part, 2].astype(BF16)
            dkv_back(2).start()

    def near_back(j):
        return remote(near_send.at[j], near_in.at[j], s_nback.at[j], r_nback.at[j], at_chip(chip - j))

    def lower_back(d):
        block = 4 * d + y
        return remote(
            near_send.at[block], near_in.at[block], s_nback.at[block], r_nback.at[block], at((z + 8 - d) % 8, y, core)
        )

    def round_back(block):
        entry = block - block % 4 + y
        return remote(
            near_send.at[block], near_in.at[entry], s_nback.at[block], r_nback.at[entry], at(z, block % 4, core)
        )

    def near_back_landed(block):
        return remote(near_send.at[0], near_in.at[block], s_nback.at[0], r_nback.at[block], sibling)

    def place_of(t):
        d, col = 2 - t // 4, t % 4
        block = (1 - core) * t + core * (4 * d + col)
        blocks = (1 - core) * t + core * (4 * d + y - col)
        return d, col, block, blocks

    def middle_sees(d, seer, col):
        blocks = 4 * d + seer - col
        return (core == 1) & (z >= d) & (blocks >= 0) & (blocks <= REACH[1][1])

    def second(t, carry):
        d, col, block, blocks = place_of(t)
        short = (core == 0) & (chip >= blocks)
        middle = (core == 1) & (z >= d) & (blocks >= 0) & (blocks <= REACH[1][1])

        @pl.when(short | middle)
        def _():
            @pl.when(((core == 0) & (blocks > 0)) | ((core == 1) & (col != y)))
            def _():
                near_landed(block).wait_recv()

            plain = (core == 1) & (blocks >= 1) & (blocks <= PLAIN[1][1])

            @pl.when(plain)
            def _():
                tile(1, y, block, 1, False, blocks)

            @pl.when(jnp.logical_not(plain))
            def _():
                tile(1, y, block, 1, True, blocks)

            for part in range(2):
                near_send[block, part] = (dkv1_acc[part, block] * scales[part]).astype(BF16)

            @pl.when((core == 0) & (blocks > 0))
            def _():
                near_back(block).start()

            @pl.when((core == 1) & (col != y))
            def _():
                round_back(block).start()

        return carry

    def join(d):
        @pl.when(core == 1)
        def _():
            for part in range(2):
                dkv1_acc[part, 4 * d + y] = dkv1_acc[part, 4 * d + y] * scales[part]

        for dy in range(1, COLUMNS):
            col = (y + dy) % 4

            @pl.when(middle_sees(d, col, y))
            def _(col=col):
                near_back_landed(4 * d + col).wait_recv()
                for part in range(2):
                    dkv1_acc[part, 4 * d + y] = dkv1_acc[part, 4 * d + y] + near_in[4 * d + col, part].astype(F32)

        if d > 0:

            @pl.when((core == 1) & (z >= d))
            def _():
                for part in range(2):
                    near_send[4 * d + y, part] = dkv1_acc[part, 4 * d + y].astype(BF16)
                lower_back(d).start()

    def nth(n):
        return n + (n // 2) * (1 - 2 * (n % 2))

    def one_column(n):
        dy = nth(n)
        col = (y + dy) % 4
        ahead = col - y
        await_queries(0, dy)
        dq_acc[0] = jnp.zeros_like(dq_acc[0])
        first = jnp.where(ahead > 0, 0, 1)
        full, end = last_block(PLAIN, 0, ahead), last_block(REACH, 0, ahead)
        large = (core == 0) & (z >= 3)
        below_count = jnp.where(large, 1 - first, jnp.maximum(full - first + 1, 0))
        above_count = jnp.where(large & (z < 7), z - 3, 0)

        @pl.when(large & (z == 7))
        def _():
            tile(0, col, 4, 4, False)

            @pl.when(n == 3)
            def _():
                for d in range(4, PLANES):
                    start_back(d)

        def plain(m, cc):
            d = jnp.where(m < below_count, first + m, 4 + m - below_count)
            tile(0, col, d, 1, False)
            return cc

        lax.fori_loop(0, below_count + above_count, plain, 0)

        def masked(d, cc):
            tile(0, col, d, 1, True)
            return cc

        lax.fori_loop(jnp.maximum(full + 1, first), end + 1, masked, 0)

        @pl.when(large)
        def _():
            tile(0, col, 1, 3, False)

        write_dq(col, 0)
        dq_copy(dy).start()


    def phase(n, carry):
        one_column(n)

        @pl.when(n == 3)
        def _():
            first_level()

            def rest_back(d, cc):
                start_back(d)
                return cc

            lax.fori_loop(4, jnp.where((core == 0) & (z < 7), z + 1, 4), rest_back, 0)

        return carry

    lax.fori_loop(1, COLUMNS, phase, 0)

    def slot_one(t, carry):
        @pl.when(t == 8)
        def _():
            second_level()
            join(2)

        second(t, 0)
        return carry

    lax.fori_loop(0, jnp.where(core == 1, 12, NEAR + 1), slot_one, 0)
    write_dq(y, 1)
    join(1)

    @pl.when(core == 0)
    def _():
        second_level()

    join(0)

    for dy in range(1, COLUMNS):
        col = (y + dy) % 4
        remote(dq_part.at[0, 0], dq_in.at[col], s_dq.at[0], r_dq.at[col], sibling).wait_recv()
    for part_half in range(2):
        half = core if part_half == 1 else other
        for g in range(GROUP):
            total = dq_part[y, 0, half, g].astype(F32)
            for dy in range(1, COLUMNS):
                total += dq_in[(y + dy) % 4, half, g].astype(F32)
            fq[part_half, 0, g] = total.astype(BF16)
            fq[part_half, 1, g] = dq_part[y, 1, half, g]
    q_fin = remote(fq.at[0], fq.at[2], s_fin.at[0], r_fin.at[0], sibling)
    q_fin.start()

    def add_near(block):
        near_back_landed(block).wait_recv()
        for part in range(2):
            dkv1_acc[part, home] = dkv1_acc[part, home] + near_in[block, part].astype(F32)

    @pl.when(core == 0)
    def _():
        dkv1_acc[0, 0] = dkv1_acc[0, 0] * SCALING

    for j in range(1, NEAR + 1):

        @pl.when(feeds(j))
        def _(j=j):
            add_near(j)

    for d in (1, 2):

        @pl.when((core == 1) & (z + d < PLANES))
        def _(d=d):
            add_near(4 * d + y)

    dkv_acc[0, 0] = dkv_acc[0, 0] * SCALING

    for d in (1, 2, 4, 5, 6, 7):

        @pl.when((z + d < PLANES) & ((core == 0) | (d < 3)))
        def _(d=d):
            dkv_landed(d).wait_recv()
            for part in range(2):
                dkv_acc[part, 0] = dkv_acc[part, 0] + dkv_in[d, part].astype(F32)

    for slot in range(2):
        for part in range(2):
            for part_half in range(2):
                half = core if part_half == 1 else other
                rows = pl.ds(pl.multiple_of(half * ROWS, ROWS), ROWS)
                acc, entry = (dkv_acc, 0) if slot == 0 else (dkv1_acc, home)
                fkv[part_half, slot, part] = acc[part, entry, rows].astype(BF16)
    kv_fin = remote(fkv.at[0], fkv.at[2], s_fin.at[1], r_fin.at[1], sibling)
    kv_fin.start()
    q_fin.wait_recv()
    kv_fin.wait_recv()

    def entry(kind):
        return 1 + (core + kind // 2) % 2

    for head in range(KV_HEADS):
        masks = [jnp.full((ROWS, HEAD_DIM), chosen_of[kind][head], jnp.int32) > 0 for kind in range(4)]

        def picked(read):
            total = jnp.zeros((ROWS, HEAD_DIM), F32)
            for kind in range(4):
                total = jnp.where(masks[kind], read(entry(kind), kind % 2).astype(F32), total)
            return total.astype(BF16)

        for g in range(GROUP):
            cols = slice((head * GROUP + g) * HEAD_DIM, (head * GROUP + g + 1) * HEAD_DIM)
            dq_out[:, cols] = picked(lambda e, slot, g=g: fq[e, slot, g])
        cols = slice(head * HEAD_DIM, (head + 1) * HEAD_DIM)
        dk_out[:, cols] = picked(lambda e, slot: fkv[e, slot, 0])
        dv_out[:, cols] = picked(lambda e, slot: fkv[e, slot, 1])

    for c in sib_copies + [q_fin, kv_fin]:
        c.wait_send()
    for half in range(2):
        for c in q_forward(0, half):
            c.wait_send()
        for way in range(2):
            st_copy(half, 0, way).wait_send()
            q_copy(half, 0, way).wait_send()
    for dy in range(1, COLUMNS):
        dq_copy(dy).wait_send()

    def sent(i, carry):
        for part in range(2):

            @pl.when(goes_up(i))
            def _(part=part):
                up_copy(i, part).wait_send()

            @pl.when(goes_down(i))
            def _(part=part):
                down_copy(i, part).wait_send()

        return carry

    lax.fori_loop(0, 5, sent, 0)

    for d in range(1, PLANES):

        @pl.when((z >= d) & ((core == 0) | (d <= UP[1])))
        def _(d=d):
            dkv_back(d).wait_send()

    for j in range(1, NEAR + 1):

        @pl.when(feeds(j))
        def _(j=j):
            near_copy(j).wait_send()

    for d in range(3):

        @pl.when(lifts(d))
        def _(d=d):
            lift_copy(d).wait_send()

        for dy in range(1, COLUMNS):

            @pl.when(rounds(d, dy))
            def _(d=d, dy=dy):
                round_copy(d, dy).wait_send()

            col = (y + dy) % 4

            @pl.when(middle_sees(d, y, col))
            def _(d=d, col=col):
                round_back(4 * d + col).wait_send()

        if d > 0:

            @pl.when((core == 1) & (z >= d))
            def _(d=d):
                lower_back(d).wait_send()

    for j in range(1, NEAR + 1):

        @pl.when(fed_by(j))
        def _(j=j):
            near_back(j).wait_send()


def per_device(queries, keys, values, outputs, out_grad, log_sum_exp, spans):
    whole = pl.BlockSpec(memory_space=pltpu.VMEM)
    dma = pltpu.SemaphoreType.DMA
    near_count = 3 * COLUMNS
    return tuple(
        pl.pallas_call(
            kernel,
            in_specs=[pl.BlockSpec(memory_space=pltpu.SMEM)] + [whole] * 6,
            out_specs=[whole] * 3,
            out_shape=[
                jax.ShapeDtypeStruct((ROWS, Q_HEADS * HEAD_DIM), BF16),
                jax.ShapeDtypeStruct((ROWS, KV_HEADS * HEAD_DIM), BF16),
                jax.ShapeDtypeStruct((ROWS, KV_HEADS * HEAD_DIM), BF16),
            ],
            scratch_shapes=[
                pltpu.VMEM((COLUMNS, 2, 2, 2, GROUP, ROWS, HEAD_DIM), BF16),
                pltpu.VMEM((PLANES, 2, 2, ROWS, HEAD_DIM), BF16),
                pltpu.VMEM((near_count, 2, 2, ROWS, HEAD_DIM), BF16),
                pltpu.VMEM((COLUMNS, 2, 2, 8, 256), F32),
                pltpu.VMEM((2, 2, GROUP, ROWS, HEAD_DIM), BF16),
                pltpu.VMEM((2, 2, ROWS, HEAD_DIM), BF16),
                pltpu.VMEM((2, 8, 256), F32),
                pltpu.VMEM((2, 2, 2, HEAD_DIM, 256), F32),
                pltpu.VMEM((2, PLANES, 256, HEAD_DIM), F32),
                pltpu.VMEM((2, near_count, 256, HEAD_DIM), F32),
                pltpu.VMEM((COLUMNS, 2, 2, GROUP, ROWS, HEAD_DIM), BF16),
                pltpu.VMEM((COLUMNS, 2, GROUP, ROWS, HEAD_DIM), BF16),
                pltpu.VMEM((PLANES, 2, 256, HEAD_DIM), BF16),
                pltpu.VMEM((PLANES, 2, 256, HEAD_DIM), BF16),
                pltpu.VMEM((near_count, 2, 256, HEAD_DIM), BF16),
                pltpu.VMEM((near_count, 2, 256, HEAD_DIM), BF16),
                pltpu.VMEM((3, 2, GROUP, ROWS, HEAD_DIM), BF16),
                pltpu.VMEM((3, 2, 2, ROWS, HEAD_DIM), BF16),
                dma((6,)),
                dma((6,)),
                dma((2, 2, 2)),
                dma((2, 2, 2)),
                dma((COLUMNS, 2, 2)),
                dma((COLUMNS, 2, 2)),
                dma((2, 2)),
                dma((2, 2)),
                dma((PLANES, 2)),
                dma((PLANES, 2)),
                dma((PLANES, 2)),
                dma((near_count,)),
                dma((near_count,)),
                dma((COLUMNS,)),
                dma((COLUMNS,)),
                dma((PLANES,)),
                dma((PLANES,)),
                dma((near_count,)),
                dma((near_count,)),
                dma((2,)),
                dma((2,)),
            ],
            compiler_params=pltpu.CompilerParams(
                collective_id=0, has_side_effects=True, vmem_limit_bytes=56 * 2**20
            ),
            name="gradients",
        )(spans, queries, keys, values, outputs, out_grad, log_sum_exp)
    )


def solution(mesh):
    in_specs = (
        P(("dp", "ctx"), None),
        P(("dp", "ctx"), None),
        P(("dp", "ctx"), None),
        P(("dp", "ctx"), None),
        P(("dp", "ctx"), None),
        P(None, ("dp", "ctx")),
        P("dp"),
    )
    out_specs = (P(("dp", "ctx"), None), P(("dp", "ctx"), None), P(("dp", "ctx"), None))
    return jax.shard_map(
        per_device, mesh=mesh, in_specs=in_specs, out_specs=out_specs, check_vma=False
    )
```

```python
import functools
import math

import jax
import jax.numpy as jnp
from jax import lax
from jax.experimental import pallas as pl
from jax.experimental.pallas import tpu as pltpu
from jax.sharding import PartitionSpec as P

Q_HEADS = 16
KV_HEADS = 4
GROUP = 4
HEAD_DIM = 128
PLANES = 8
COLUMNS = 4
ROWS = 128
SCALING = 1.0 / math.sqrt(HEAD_DIM)
LOG2E = math.log2(math.e)
BF16 = jnp.bfloat16
F32 = jnp.float32
MESH = pl.DeviceIdType.MESH
NT = (((1,), (1,)), ((), ()))
NN = (((1,), (0,)), ((), ()))
CHIPS = PLANES * COLUMNS
REACH = ((31, 2), (16, 8))
PLAIN = ((31, 0), (7, 3))
UP = (3, 4)
DOWN = 4
NEAR = 2


def dot(a, b, dims=NN):
    return lax.dot_general(a, b, dims, preferred_element_type=F32)


def place():
    me = lax.axis_index("ctx")
    return me // 8, (me // 2) % 4, me % 2


def at(z, y, core):
    return {"ctx": z * 8 + y * 2 + core}


def remote(src, dst, send, recv, device):
    return pltpu.make_async_remote_copy(
        src_ref=src, dst_ref=dst, send_sem=send, recv_sem=recv, device_id=device, device_id_type=MESH
    )


def by_class(table, core, slot):
    first, second = table
    low = first[0] + (first[1] - first[0]) * slot
    high = second[0] + (second[1] - second[0]) * slot
    return low + (high - low) * core


def kernel(
    spans_ref,
    q_ref,
    k_ref,
    v_ref,
    o_ref,
    g_ref,
    lse_ref,
    dq_out,
    dk_out,
    dv_out,
    qd,
    kv,
    kv1,
    st,
    q_sib,
    kv_sib,
    st_sib,
    dq_acc,
    dkv_acc,
    dkv1_acc,
    dq_part,
    dq_in,
    dkv_send,
    dkv_in,
    near_send,
    near_in,
    fq,
    fkv,
    s_sib,
    r_sib,
    s_q,
    s_st,
    r_q,
    r_st,
    s_fq,
    s_fst,
    s_up,
    s_down,
    r_kv,
    s_near,
    r_near,
    s_dq,
    r_dq,
    s_dkv,
    r_dkv,
    s_nback,
    r_nback,
    s_fin,
    r_fin,
):
    z, y, core = place()
    other = 1 - core
    up_reach = UP[0] + (UP[1] - UP[0]) * core
    chip = z * COLUMNS + y
    home = y * core
    sibling = at(z, y, other)
    before, after, across = (y + 3) % 4, (y + 1) % 4, (y + 2) % 4
    left, right, far = at(z, before, core), at(z, after, core), at(z, across, core)
    above, below = at((z + 1) % 8, y, core), at((z + 7) % 8, y, core)

    def at_chip(number):
        return at(number // COLUMNS, number % COLUMNS, core)

    def feeds(j):
        return (core == 0) & (chip + j < CHIPS)

    def fed_by(j):
        return (core == 0) & (chip >= j)

    barrier = pltpu.get_barrier_semaphore()
    for peer in (sibling, left, right, far):
        pl.semaphore_signal(barrier, inc=1, device_id=peer, device_id_type=MESH)
    for dz in range(1, PLANES):
        pl.semaphore_signal(barrier, inc=1, device_id=at((z + dz) % 8, y, core), device_id_type=MESH)
    for j in range(1, NEAR + 1):

        @pl.when(feeds(j))
        def _(j=j):
            pl.semaphore_signal(barrier, inc=1, device_id=at_chip(chip + j), device_id_type=MESH)

        @pl.when(fed_by(j))
        def _(j=j):
            pl.semaphore_signal(barrier, inc=1, device_id=at_chip(chip - j), device_id_type=MESH)

    greetings = 11 + (1 - core) * (jnp.minimum(NEAR, chip) + jnp.minimum(NEAR, CHIPS - 1 - chip))

    spans = [spans_ref[i] for i in range(KV_HEADS)]
    tops = ((4096, 8192), (0, 512), (2048, 4096), (1024, 2048))
    chosen_of, limits = [], []
    for low, top in tops:
        picks = [jnp.where((span > low) & (span <= top), 1, 0) for span in spans]
        chosen_of.append(picks)
        limits.append(sum(pick * span for pick, span in zip(picks, spans)))

    def taker(picks):
        weights = [pick.astype(F32) for pick in picks]

        def taken(ref, g, width):
            total = None
            for head in range(KV_HEADS):
                first = head * width + g * HEAD_DIM
                term = ref[:, first : first + HEAD_DIM] * weights[head].astype(BF16)
                total = term if total is None else total + term
            return total

        return weights, taken

    def pack_queries(picks, q_to, st_to):
        weights, taken = taker(picks)
        st_to[...] = jnp.zeros((8, 256), F32)
        for g in range(GROUP):
            grad = taken(g_ref, g, 512)
            q_to[0, g] = taken(q_ref, g, 512)
            q_to[1, g] = grad
            product = grad.astype(F32) * taken(o_ref, g, 512).astype(F32)
            lanes = slice((g % 2) * ROWS, (g % 2 + 1) * ROWS)
            lse = sum(
                lse_ref[head * GROUP + g : head * GROUP + g + 1, :] * weights[head] for head in range(KV_HEADS)
            )
            st_to[g // 2 : g // 2 + 1, lanes] = lse * LOG2E
            st_to[2 + g // 2 : 3 + g // 2, lanes] = jnp.sum(product.T, axis=0, keepdims=True)

    def pack_keys(picks, kv_to):
        taken = taker(picks)[1]
        kv_to[0] = taken(k_ref, 0, HEAD_DIM)
        kv_to[1] = taken(v_ref, 0, HEAD_DIM)

    theirs = [
        [jnp.where(core == 0, a, b) for a, b in zip(chosen_of[2 + slot], chosen_of[slot])] for slot in range(2)
    ]
    ours = [[jnp.where(core == 0, a, b) for a, b in zip(chosen_of[slot], chosen_of[2 + slot])] for slot in range(2)]

    def q_copy(half, slot, way):
        return remote(
            qd.at[y, half, slot],
            qd.at[y, half, slot],
            s_q.at[half, slot, way],
            r_q.at[y, half, slot],
            right if way == 0 else left,
        )

    def st_copy(half, slot, way):
        return remote(
            st.at[y, half, slot],
            st.at[y, half, slot],
            s_st.at[half, slot, way],
            r_st.at[y, half, slot],
            right if way == 0 else left,
        )

    def start_q(half, slot):
        for way in range(2):
            st_copy(half, slot, way).start()
            q_copy(half, slot, way).start()

    sib_copies = [
        remote(kv_sib.at[0], kv.at[0, core], s_sib.at[4], r_sib.at[4], sibling),
    ]
    for slot in range(2):
        sib_copies.append(remote(q_sib.at[slot], qd.at[y, core, slot], s_sib.at[slot], r_sib.at[slot], sibling))
        sib_copies.append(
            remote(st_sib.at[slot], st.at[y, core, slot], s_sib.at[2 + slot], r_sib.at[2 + slot], sibling)
        )

    sib_copies.append(remote(kv_sib.at[1], kv1.at[y * other, core], s_sib.at[5], r_sib.at[5], sibling))

    for slot in range(2):
        pack_keys(theirs[slot], kv_sib.at[slot])
    pack_queries(ours[0], qd.at[y, core, 0], st.at[y, core, 0])
    pl.semaphore_wait(barrier, greetings)
    start_q(core, 0)
    sib_copies[0].start()
    sib_copies[5].start()
    pack_keys(ours[0], kv.at[0, core])
    pack_keys(ours[1], kv1.at[home, core])
    pack_queries(theirs[0], q_sib.at[0], st_sib.at[0])
    sib_copies[1].start()
    sib_copies[2].start()

    def up_copy(d, part):
        return remote(
            kv.at[d, :, part], kv.at[d + 1, :, part], s_up.at[d, part], r_kv.at[d + 1, part], above
        )

    def down_copy(e, part):
        return remote(
            kv.at[(8 - e) % 8, :, part], kv.at[7 - e, :, part], s_down.at[e, part], r_kv.at[7 - e, part], below
        )

    def goes_up(d):
        return (z + 1 < PLANES) & (z >= d) & (d < up_reach)

    def goes_down(e):
        return (core == 0) & (e < DOWN) & ((z + e) % 8 < DOWN)

    def kv_landed(d, part):
        return remote(kv.at[0, :, 0], kv.at[d, :, part], s_up.at[0, 0], r_kv.at[d, part], sibling)

    def hop(i):
        for part in range(2):
            if not isinstance(i, int):

                @pl.when((z >= i) & (i <= up_reach))
                def _(part=part):
                    kv_landed(i, part).wait_recv()

            @pl.when(goes_up(i))
            def _(part=part):
                up_copy(i, part).start()

            if not isinstance(i, int):

                @pl.when((core == 0) & ((z + i) % 8 < DOWN))
                def _(part=part):
                    kv_landed(8 - i, part).wait_recv()

            @pl.when(goes_down(i))
            def _(part=part):
                down_copy(i, part).start()

    def near_copy(j):
        return remote(kv1.at[0], kv1.at[j], s_near.at[j], r_near.at[j], at_chip(chip + j))

    def lift_copy(d):
        return remote(kv1.at[4 * d + y], kv1.at[4 * d + 4 + y], s_near.at[d], r_near.at[4 * d + 4 + y], above)

    def round_copy(d, dy):
        block = 4 * d + y
        return remote(kv1.at[block], kv1.at[block], s_near.at[3 * d + dy + 2], r_near.at[block], at(z, (y + dy) % 4, core))

    def near_landed(block):
        return remote(kv1.at[0], kv1.at[block], s_near.at[0], r_near.at[block], sibling)

    def lifts(d):
        return (core == 1) & (d < 2) & (z >= d) & (z + 1 < PLANES)

    def rounds(d, dy):
        col = (y + dy) % 4
        blocks = 4 * d + col - y
        return (core == 1) & (z >= d) & (blocks >= 0) & (blocks <= REACH[1][1])

    def lift(d):
        if d > 0:

            @pl.when((core == 1) & (z >= d))
            def _():
                near_landed(4 * d + y).wait_recv()

        if d < 2:

            @pl.when(lifts(d))
            def _():
                lift_copy(d).start()

    def start_near():
        for j in range(1, NEAR + 1):

            @pl.when(feeds(j))
            def _(j=j):
                near_copy(j).start()

    def start_rounds():
        for d in range(3):
            for dy in (1, 3, 2):

                @pl.when(rounds(d, dy))
                def _(d=d, dy=dy):
                    round_copy(d, dy).start()

    sib_copies[0].wait_recv()
    hop(0)
    sib_copies[5].wait_recv()
    lift(0)
    start_near()
    pack_queries(theirs[1], q_sib.at[1], st_sib.at[1])
    sib_copies[3].start()
    sib_copies[4].start()
    sib_copies[1].wait_recv()
    sib_copies[2].wait_recv()
    start_q(other, 0)
    pack_queries(ours[1], qd.at[y, core, 1], st.at[y, core, 1])

    dkv_acc[...] = jnp.zeros_like(dkv_acc)
    dkv1_acc[...] = jnp.zeros_like(dkv1_acc)
    own_limits = [jnp.where(core == 0, limits[slot], limits[2 + slot]) for slot in range(2)]

    def tile(slot, col, d0, count, masked, blocks=0):
        size = count * 256
        keys, acc = (kv, dkv_acc) if slot == 0 else (kv1, dkv1_acc)
        into = pl.ds(d0, count)
        k = keys[pl.ds(d0, count), :, 0].reshape(size, HEAD_DIM)
        v = keys[pl.ds(d0, count), :, 1].reshape(size, HEAD_DIM)
        k_t = k.T
        base = d0 * 1024 + (col - y) * 256 if slot == 0 else blocks * 256
        if count == 1:
            groups = [[(half, pair) for half in range(2) for pair in range(2)]]
        else:
            groups = [[(half, pair)] for half in range(2) for pair in range(2)]
        for group in groups:
            width = 256 * len(group)

            def rows(what, group=group, width=width):
                return jnp.concatenate(
                    [
                        qd[col, half, slot, what, 2 * pair : 2 * pair + 2].reshape(256, HEAD_DIM)
                        for half, pair in group
                    ],
                    axis=0,
                )

            def stats(first, group=group):
                return jnp.concatenate(
                    [st[col, half, slot, first + pair : first + pair + 1] for half, pair in group], axis=1
                )

            q, g = rows(0), rows(1)
            prob = jnp.exp2(dot(k, q, NT) * (SCALING * LOG2E) - stats(0))
            if masked:
                key = lax.broadcasted_iota(jnp.int32, (size, width), 0)
                lane = lax.broadcasted_iota(jnp.int32, (size, width), 1)
                row = lane % ROWS + lane // 512 * ROWS
                distance = row - key + base
                prob = jnp.where((distance >= 0) & (distance < own_limits[slot]), prob, 0.0)
            ds = (prob * (dot(v, g, NT) - stats(2))).astype(BF16)
            low = prob.astype(BF16)
            acc[0, into] += dot(ds, q).reshape(count, 256, HEAD_DIM)
            acc[1, into] += dot(low, g).reshape(count, 256, HEAD_DIM)
            change = dot(k_t, ds)
            for n, (half, pair) in enumerate(group):
                dq_acc[slot, half, pair] += change[:, n * 256 : (n + 1) * 256]

    def last_block(table, slot, ahead):
        return jnp.minimum(z, (by_class(table, core, slot) - ahead + 4) // 4 - 1)

    def write_dq(col, slot):
        for half in range(2):
            for pair in range(2):
                total = dq_acc[slot, half, pair].T * SCALING
                dq_part[col, slot, half, 2 * pair : 2 * pair + 2] = total.reshape(2, ROWS, HEAD_DIM).astype(BF16)

    def q_landed(col, half, slot):
        return remote(qd.at[0, 0, 0], qd.at[col, half, slot], s_q.at[0, 0, 0], r_q.at[col, half, slot], sibling)

    def st_landed(col, half, slot):
        return remote(st.at[0, 0, 0], st.at[col, half, slot], s_st.at[0, 0, 0], r_st.at[col, half, slot], sibling)

    def q_forward(slot, half):
        col, to = (before, right) if half == 0 else (after, left)
        return (
            remote(
                st.at[col, half, slot], st.at[col, half, slot], s_fst.at[slot, half], r_st.at[col, half, slot], to
            ),
            remote(qd.at[col, half, slot], qd.at[col, half, slot], s_fq.at[slot, half], r_q.at[col, half, slot], to),
        )

    def pass_queries(slot, which):
        for half in range(2):

            @pl.when(which == half)
            def _(half=half):
                col = before if half == 0 else after
                st_landed(col, half, slot).wait_recv()
                q_landed(col, half, slot).wait_recv()
                for c in q_forward(slot, half):
                    c.start()

    def await_queries(slot, dy):
        col = (y + dy) % 4
        for half in range(2):

            @pl.when((dy != 3) if half == 0 else (dy != 1))
            def _(half=half):
                st_landed(col, half, slot).wait_recv()
                q_landed(col, half, slot).wait_recv()

    scales = (SCALING, 1.0)

    def dkv_landed(d):
        return remote(dkv_send.at[0], dkv_in.at[d], s_dkv.at[0], r_dkv.at[d], sibling)

    def dkv_back(d):
        return remote(dkv_send.at[d], dkv_in.at[d], s_dkv.at[d], r_dkv.at[d], at((z + 8 - d) % 8, y, core))

    def dkv_join(d):
        return remote(dkv_send.at[d], dkv_in.at[d], s_dkv.at[d], r_dkv.at[d], at((z + 10 - d) % 8, y, core))

    def ready(d):
        for part in range(2):
            dkv_send[d, part] = (dkv_acc[part, d] * scales[part]).astype(BF16)

    def start_back(d):
        ready(d)
        dkv_back(d).start()

    def first_level():
        @pl.when((core == 1) & (z >= 4))
        def _():
            ready(4)
            dkv_join(4).start()

        @pl.when(z >= 3)
        def _():
            ready(3)
            dkv_join(3).start()

        @pl.when(z >= 1)
        def _():
            start_back(1)

    def second_level():
        @pl.when(z >= 2)
        def _():
            for part in range(2):
                dkv_acc[part, 2] = dkv_acc[part, 2] * scales[part]

            for d in (3, 4):

                @pl.when((z + d - 2 < PLANES) & (core >= d - 3))
                def _(d=d):
                    dkv_landed(d).wait_recv()
                    for part in range(2):
                        dkv_acc[part, 2] = dkv_acc[part, 2] + dkv_in[d, part].astype(F32)

            for part in range(2):
                dkv_send[2, part] = dkv_acc[part, 2].astype(BF16)
            dkv_back(2).start()

    def near_back(j):
        return remote(near_send.at[j], near_in.at[j], s_nback.at[j], r_nback.at[j], at_chip(chip - j))

    def lower_back(d):
        block = 4 * d + y
        return remote(
            near_send.at[block], near_in.at[block], s_nback.at[block], r_nback.at[block], at((z + 8 - d) % 8, y, core)
        )

    def round_back(block):
        entry = block - block % 4 + y
        return remote(
            near_send.at[block], near_in.at[entry], s_nback.at[block], r_nback.at[entry], at(z, block % 4, core)
        )

    def near_back_landed(block):
        return remote(near_send.at[0], near_in.at[block], s_nback.at[0], r_nback.at[block], sibling)

    def place_of(t):
        d, col = 2 - t // 4, t % 4
        block = (1 - core) * t + core * (4 * d + col)
        blocks = (1 - core) * t + core * (4 * d + y - col)
        return d, col, block, blocks

    def middle_sees(d, seer, col):
        blocks = 4 * d + seer - col
        return (core == 1) & (z >= d) & (blocks >= 0) & (blocks <= REACH[1][1])

    def second(t, carry):
        d, col, block, blocks = place_of(t)
        short = (core == 0) & (chip >= blocks)
        middle = (core == 1) & (z >= d) & (blocks >= 0) & (blocks <= REACH[1][1])

        @pl.when(short | middle)
        def _():
            @pl.when(((core == 0) & (blocks > 0)) | ((core == 1) & (col != y)))
            def _():
                near_landed(block).wait_recv()

            plain = (core == 1) & (blocks >= 1) & (blocks <= PLAIN[1][1])

            @pl.when(plain)
            def _():
                tile(1, y, block, 1, False, blocks)

            @pl.when(jnp.logical_not(plain))
            def _():
                tile(1, y, block, 1, True, blocks)

            for part in range(2):
                near_send[block, part] = (dkv1_acc[part, block] * scales[part]).astype(BF16)

            @pl.when((core == 0) & (blocks > 0))
            def _():
                near_back(block).start()

            @pl.when((core == 1) & (col != y))
            def _():
                round_back(block).start()

        return carry

    dq_acc[...] = jnp.zeros_like(dq_acc)
    tile(0, y, 0, 1, True)

    def step(i, carry):
        @pl.when(i == 3)
        def _():
            pass_queries(0, core)

        @pl.when(i == 4)
        def _():
            pass_queries(0, other)

        hop(i)

        @pl.when(i == 1)
        def _():
            sib_copies[3].wait_recv()
            sib_copies[4].wait_recv()

        @pl.when(i == 2)
        def _():
            lift(1)

        @pl.when(i == 3)
        def _():
            lift(2)

        @pl.when(i == 4)
        def _():
            start_rounds()

        full, end = last_block(PLAIN, 0, 0), last_block(REACH, 0, 0)
        here = (i <= up_reach) & (i <= end)

        @pl.when(here & (i <= full))
        def _():
            tile(0, y, i, 1, False)

        @pl.when(here & (i > full))
        def _():
            tile(0, y, i, 1, True)

        @pl.when((core == 0) & (z >= 8 - i))
        def _():
            tile(0, y, 8 - i, 1, False)

        @pl.when(i < 4)
        def _():
            second((1 - core) * (i - 1) + core * (4 * (3 - i) + y), 0)

        return carry

    lax.fori_loop(1, 5, step, 0)
    write_dq(y, 0)

    def dq_copy(dy):
        col = (y + dy) % 4
        return remote(dq_part.at[col, 0], dq_in.at[y], s_dq.at[dy], r_dq.at[y], at(z, col, core))

    def join(d):
        @pl.when(core == 1)
        def _():
            for part in range(2):
                dkv1_acc[part, 4 * d + y] = dkv1_acc[part, 4 * d + y] * scales[part]

        for dy in range(1, COLUMNS):
            col = (y + dy) % 4

            @pl.when(middle_sees(d, col, y))
            def _(col=col):
                near_back_landed(4 * d + col).wait_recv()
                for part in range(2):
                    dkv1_acc[part, 4 * d + y] = dkv1_acc[part, 4 * d + y] + near_in[4 * d + col, part].astype(F32)

        if d > 0:

            @pl.when((core == 1) & (z >= d))
            def _():
                for part in range(2):
                    near_send[4 * d + y, part] = dkv1_acc[part, 4 * d + y].astype(BF16)
                lower_back(d).start()

    def nth(n):
        return n + (n // 2) * (1 - 2 * (n % 2))

    def one_column(n):
        dy = nth(n)
        col = (y + dy) % 4
        ahead = col - y
        await_queries(0, dy)
        dq_acc[0] = jnp.zeros_like(dq_acc[0])
        first = jnp.where(ahead > 0, 0, 1)
        full, end = last_block(PLAIN, 0, ahead), last_block(REACH, 0, ahead)
        large = (core == 0) & (z >= 3)
        below_count = jnp.where(large, 1 - first, jnp.maximum(full - first + 1, 0))
        above_count = jnp.where(large & (z < 7), z - 3, 0)

        @pl.when(large & (z == 7))
        def _():
            tile(0, col, 4, 4, False)

            @pl.when(n == 3)
            def _():
                for d in range(4, PLANES):
                    start_back(d)

        def plain(m, cc):
            d = jnp.where(m < below_count, first + m, 4 + m - below_count)
            tile(0, col, d, 1, False)
            return cc

        lax.fori_loop(0, below_count + above_count, plain, 0)

        def masked(d, cc):
            tile(0, col, d, 1, True)
            return cc

        lax.fori_loop(jnp.maximum(full + 1, first), end + 1, masked, 0)

        @pl.when(large)
        def _():
            tile(0, col, 1, 3, False)

        write_dq(col, 0)
        dq_copy(dy).start()


    def phase(n, carry):
        one_column(n)

        @pl.when(n == 3)
        def _():
            first_level()

            def rest_back(d, cc):
                start_back(d)
                return cc

            lax.fori_loop(4, jnp.where((core == 0) & (z < 7), z + 1, 4), rest_back, 0)

        return carry

    lax.fori_loop(1, COLUMNS, phase, 0)

    def slot_one(t, carry):
        @pl.when(t == 8)
        def _():
            second_level()
            join(2)

        @pl.when(t % 4 != y)
        def _():
            second(t, 0)

        return carry

    lax.fori_loop(0, 12 * core, slot_one, 0)
    join(1)

    @pl.when(core == 0)
    def _():
        second_level()

    write_dq(y, 1)
    join(0)

    def fin(ref, slot, n):
        return remote(ref.at[0, slot], ref.at[2, slot], s_fin.at[n, slot], r_fin.at[n, slot], sibling)

    for part_half in range(2):
        half = core if part_half == 1 else other
        for g in range(GROUP):
            fq[part_half, 1, g] = dq_part[y, 1, half, g]
    fin(fq, 1, 0).start()
    for dy in range(1, COLUMNS):
        col = (y + dy) % 4
        remote(dq_part.at[0, 0], dq_in.at[col], s_dq.at[0], r_dq.at[col], sibling).wait_recv()
    for part_half in range(2):
        half = core if part_half == 1 else other
        for g in range(GROUP):
            total = dq_part[y, 0, half, g].astype(F32)
            for dy in range(1, COLUMNS):
                total += dq_in[(y + dy) % 4, half, g].astype(F32)
            fq[part_half, 0, g] = total.astype(BF16)
    fin(fq, 0, 0).start()

    def add_near(block):
        near_back_landed(block).wait_recv()
        for part in range(2):
            dkv1_acc[part, home] = dkv1_acc[part, home] + near_in[block, part].astype(F32)

    @pl.when(core == 0)
    def _():
        dkv1_acc[0, 0] = dkv1_acc[0, 0] * SCALING

    for j in range(1, NEAR + 1):

        @pl.when(feeds(j))
        def _(j=j):
            add_near(j)

    for d in (1, 2):

        @pl.when((core == 1) & (z + d < PLANES))
        def _(d=d):
            add_near(4 * d + y)

    dkv_acc[0, 0] = dkv_acc[0, 0] * SCALING

    for d in (1, 2, 4, 5, 6, 7):

        @pl.when((z + d < PLANES) & ((core == 0) | (d < 3)))
        def _(d=d):
            dkv_landed(d).wait_recv()
            for part in range(2):
                dkv_acc[part, 0] = dkv_acc[part, 0] + dkv_in[d, part].astype(F32)

    for slot in range(2):
        for part in range(2):
            for part_half in range(2):
                half = core if part_half == 1 else other
                rows = pl.ds(pl.multiple_of(half * ROWS, ROWS), ROWS)
                acc, entry = (dkv_acc, 0) if slot == 0 else (dkv1_acc, home)
                fkv[part_half, slot, part] = acc[part, entry, rows].astype(BF16)
        fin(fkv, slot, 1).start()
    for slot in range(2):
        fin(fq, slot, 0).wait_recv()

    def entry(kind):
        return 1 + (core + kind // 2) % 2

    def place_head(head, what):
        masks = [jnp.full((ROWS, HEAD_DIM), chosen_of[kind][head], jnp.int32) > 0 for kind in range(4)]

        def picked(read):
            total = jnp.zeros((ROWS, HEAD_DIM), F32)
            for kind in range(4):
                total = jnp.where(masks[kind], read(entry(kind), kind % 2).astype(F32), total)
            return total.astype(BF16)

        if what == 0:
            for g in range(GROUP):
                cols = slice((head * GROUP + g) * HEAD_DIM, (head * GROUP + g + 1) * HEAD_DIM)
                dq_out[:, cols] = picked(lambda e, slot, g=g: fq[e, slot, g])
        else:
            cols = slice(head * HEAD_DIM, (head + 1) * HEAD_DIM)
            dk_out[:, cols] = picked(lambda e, slot: fkv[e, slot, 0])
            dv_out[:, cols] = picked(lambda e, slot: fkv[e, slot, 1])

    for head in range(KV_HEADS):
        place_head(head, 0)
    for slot in range(2):
        fin(fkv, slot, 1).wait_recv()
    for head in range(KV_HEADS):
        place_head(head, 1)

    for c in sib_copies:
        c.wait_send()
    for slot in range(2):
        fin(fq, slot, 0).wait_send()
        fin(fkv, slot, 1).wait_send()
    for half in range(2):
        for c in q_forward(0, half):
            c.wait_send()
        for way in range(2):
            st_copy(half, 0, way).wait_send()
            q_copy(half, 0, way).wait_send()
    for dy in range(1, COLUMNS):
        dq_copy(dy).wait_send()

    def sent(i, carry):
        for part in range(2):

            @pl.when(goes_up(i))
            def _(part=part):
                up_copy(i, part).wait_send()

            @pl.when(goes_down(i))
            def _(part=part):
                down_copy(i, part).wait_send()

        return carry

    lax.fori_loop(0, 5, sent, 0)

    for d in range(1, PLANES):

        @pl.when((z >= d) & ((core == 0) | (d <= UP[1])))
        def _(d=d):
            dkv_back(d).wait_send()

    for j in range(1, NEAR + 1):

        @pl.when(feeds(j))
        def _(j=j):
            near_copy(j).wait_send()

    for d in range(3):

        @pl.when(lifts(d))
        def _(d=d):
            lift_copy(d).wait_send()

        for dy in range(1, COLUMNS):

            @pl.when(rounds(d, dy))
            def _(d=d, dy=dy):
                round_copy(d, dy).wait_send()

            col = (y + dy) % 4

            @pl.when(middle_sees(d, y, col))
            def _(d=d, col=col):
                round_back(4 * d + col).wait_send()

        if d > 0:

            @pl.when((core == 1) & (z >= d))
            def _(d=d):
                lower_back(d).wait_send()

    for j in range(1, NEAR + 1):

        @pl.when(fed_by(j))
        def _(j=j):
            near_back(j).wait_send()


def per_device(queries, keys, values, outputs, out_grad, log_sum_exp, spans):
    whole = pl.BlockSpec(memory_space=pltpu.VMEM)
    dma = pltpu.SemaphoreType.DMA
    near_count = 3 * COLUMNS
    return tuple(
        pl.pallas_call(
            kernel,
            in_specs=[pl.BlockSpec(memory_space=pltpu.SMEM)] + [whole] * 6,
            out_specs=[whole] * 3,
            out_shape=[
                jax.ShapeDtypeStruct((ROWS, Q_HEADS * HEAD_DIM), BF16),
                jax.ShapeDtypeStruct((ROWS, KV_HEADS * HEAD_DIM), BF16),
                jax.ShapeDtypeStruct((ROWS, KV_HEADS * HEAD_DIM), BF16),
            ],
            scratch_shapes=[
                pltpu.VMEM((COLUMNS, 2, 2, 2, GROUP, ROWS, HEAD_DIM), BF16),
                pltpu.VMEM((PLANES, 2, 2, ROWS, HEAD_DIM), BF16),
                pltpu.VMEM((near_count, 2, 2, ROWS, HEAD_DIM), BF16),
                pltpu.VMEM((COLUMNS, 2, 2, 8, 256), F32),
                pltpu.VMEM((2, 2, GROUP, ROWS, HEAD_DIM), BF16),
                pltpu.VMEM((2, 2, ROWS, HEAD_DIM), BF16),
                pltpu.VMEM((2, 8, 256), F32),
                pltpu.VMEM((2, 2, 2, HEAD_DIM, 256), F32),
                pltpu.VMEM((2, PLANES, 256, HEAD_DIM), F32),
                pltpu.VMEM((2, near_count, 256, HEAD_DIM), F32),
                pltpu.VMEM((COLUMNS, 2, 2, GROUP, ROWS, HEAD_DIM), BF16),
                pltpu.VMEM((COLUMNS, 2, GROUP, ROWS, HEAD_DIM), BF16),
                pltpu.VMEM((PLANES, 2, 256, HEAD_DIM), BF16),
                pltpu.VMEM((PLANES, 2, 256, HEAD_DIM), BF16),
                pltpu.VMEM((near_count, 2, 256, HEAD_DIM), BF16),
                pltpu.VMEM((near_count, 2, 256, HEAD_DIM), BF16),
                pltpu.VMEM((3, 2, GROUP, ROWS, HEAD_DIM), BF16),
                pltpu.VMEM((3, 2, 2, ROWS, HEAD_DIM), BF16),
                dma((6,)),
                dma((6,)),
                dma((2, 2, 2)),
                dma((2, 2, 2)),
                dma((COLUMNS, 2, 2)),
                dma((COLUMNS, 2, 2)),
                dma((2, 2)),
                dma((2, 2)),
                dma((PLANES, 2)),
                dma((PLANES, 2)),
                dma((PLANES, 2)),
                dma((near_count,)),
                dma((near_count,)),
                dma((COLUMNS,)),
                dma((COLUMNS,)),
                dma((PLANES,)),
                dma((PLANES,)),
                dma((near_count,)),
                dma((near_count,)),
                dma((2, 2)),
                dma((2, 2)),
            ],
            compiler_params=pltpu.CompilerParams(
                collective_id=0, has_side_effects=True, vmem_limit_bytes=56 * 2**20
            ),
            name="gradients",
        )(spans, queries, keys, values, outputs, out_grad, log_sum_exp)
    )


def solution(mesh):
    in_specs = (
        P(("dp", "ctx"), None),
        P(("dp", "ctx"), None),
        P(("dp", "ctx"), None),
        P(("dp", "ctx"), None),
        P(("dp", "ctx"), None),
        P(None, ("dp", "ctx")),
        P("dp"),
    )
    out_specs = (P(("dp", "ctx"), None), P(("dp", "ctx"), None), P(("dp", "ctx"), None))
    return jax.shard_map(
        per_device, mesh=mesh, in_specs=in_specs, out_specs=out_specs, check_vma=False
    )
```

```python
import functools
import math

import jax
import jax.numpy as jnp
from jax import lax
from jax.experimental import pallas as pl
from jax.experimental.pallas import tpu as pltpu
from jax.sharding import PartitionSpec as P

Q_HEADS = 16
KV_HEADS = 4
GROUP = 4
HEAD_DIM = 128
PLANES = 8
COLUMNS = 4
ROWS = 128
SCALING = 1.0 / math.sqrt(HEAD_DIM)
LOG2E = math.log2(math.e)
BF16 = jnp.bfloat16
F32 = jnp.float32
MESH = pl.DeviceIdType.MESH
NT = (((1,), (1,)), ((), ()))
NN = (((1,), (0,)), ((), ()))
CHIPS = PLANES * COLUMNS
REACH = ((31, 2), (16, 8))
PLAIN = ((31, 0), (7, 3))
UP = (3, 4)
DOWN = 4
NEAR = 2


def dot(a, b, dims=NN):
    return lax.dot_general(a, b, dims, preferred_element_type=F32)


def place():
    me = lax.axis_index("ctx")
    return me // 8, (me // 2) % 4, me % 2


def at(z, y, core):
    return {"ctx": z * 8 + y * 2 + core}


def remote(src, dst, send, recv, device):
    return pltpu.make_async_remote_copy(
        src_ref=src, dst_ref=dst, send_sem=send, recv_sem=recv, device_id=device, device_id_type=MESH
    )


def by_class(table, core, slot):
    first, second = table
    low = first[0] + (first[1] - first[0]) * slot
    high = second[0] + (second[1] - second[0]) * slot
    return low + (high - low) * core


def kernel(
    spans_ref,
    q_ref,
    k_ref,
    v_ref,
    o_ref,
    g_ref,
    lse_ref,
    dq_out,
    dk_out,
    dv_out,
    qd,
    kv,
    kv1,
    st,
    q_sib,
    kv_sib,
    st_sib,
    dq_acc,
    dkv_acc,
    dkv1_acc,
    dq_part,
    dq_in,
    dkv_send,
    dkv_in,
    near_send,
    near_in,
    fq,
    fkv,
    s_sib,
    r_sib,
    s_q,
    s_st,
    r_q,
    r_st,
    s_fq,
    s_fst,
    s_up,
    s_down,
    r_kv,
    s_near,
    r_near,
    s_dq,
    r_dq,
    s_dkv,
    r_dkv,
    s_nback,
    r_nback,
    s_fin,
    r_fin,
):
    z, y, core = place()
    other = 1 - core
    up_reach = UP[0] + (UP[1] - UP[0]) * core
    chip = z * COLUMNS + y
    home = y * core
    sibling = at(z, y, other)
    before, after, across = (y + 3) % 4, (y + 1) % 4, (y + 2) % 4
    left, right, far = at(z, before, core), at(z, after, core), at(z, across, core)
    above, below = at((z + 1) % 8, y, core), at((z + 7) % 8, y, core)

    def at_chip(number):
        return at(number // COLUMNS, number % COLUMNS, core)

    def feeds(j):
        return (core == 0) & (chip + j < CHIPS)

    def fed_by(j):
        return (core == 0) & (chip >= j)

    barrier = pltpu.get_barrier_semaphore()
    for peer in (sibling, left, right, far):
        pl.semaphore_signal(barrier, inc=1, device_id=peer, device_id_type=MESH)
    for dz in range(1, PLANES):
        pl.semaphore_signal(barrier, inc=1, device_id=at((z + dz) % 8, y, core), device_id_type=MESH)
    for j in range(1, NEAR + 1):

        @pl.when(feeds(j))
        def _(j=j):
            pl.semaphore_signal(barrier, inc=1, device_id=at_chip(chip + j), device_id_type=MESH)

        @pl.when(fed_by(j))
        def _(j=j):
            pl.semaphore_signal(barrier, inc=1, device_id=at_chip(chip - j), device_id_type=MESH)

    greetings = 11 + (1 - core) * (jnp.minimum(NEAR, chip) + jnp.minimum(NEAR, CHIPS - 1 - chip))

    spans = [spans_ref[i] for i in range(KV_HEADS)]
    tops = ((4096, 8192), (0, 512), (2048, 4096), (1024, 2048))
    chosen_of, limits = [], []
    for low, top in tops:
        picks = [jnp.where((span > low) & (span <= top), 1, 0) for span in spans]
        chosen_of.append(picks)
        limits.append(sum(pick * span for pick, span in zip(picks, spans)))

    def taker(picks):
        weights = [pick.astype(F32) for pick in picks]

        def taken(ref, g, width):
            total = None
            for head in range(KV_HEADS):
                first = head * width + g * HEAD_DIM
                term = ref[:, first : first + HEAD_DIM] * weights[head].astype(BF16)
                total = term if total is None else total + term
            return total

        return weights, taken

    def pack_queries(picks, q_to, st_to):
        weights, taken = taker(picks)
        st_to[...] = jnp.zeros((8, 256), F32)
        for g in range(GROUP):
            grad = taken(g_ref, g, 512)
            q_to[0, g] = taken(q_ref, g, 512)
            q_to[1, g] = grad
            product = grad.astype(F32) * taken(o_ref, g, 512).astype(F32)
            lanes = slice((g % 2) * ROWS, (g % 2 + 1) * ROWS)
            lse = sum(
                lse_ref[head * GROUP + g : head * GROUP + g + 1, :] * weights[head] for head in range(KV_HEADS)
            )
            st_to[g // 2 : g // 2 + 1, lanes] = lse * LOG2E
            st_to[2 + g // 2 : 3 + g // 2, lanes] = jnp.sum(product.T, axis=0, keepdims=True)

    def pack_keys(picks, kv_to):
        taken = taker(picks)[1]
        kv_to[0] = taken(k_ref, 0, HEAD_DIM)
        kv_to[1] = taken(v_ref, 0, HEAD_DIM)

    theirs = [
        [jnp.where(core == 0, a, b) for a, b in zip(chosen_of[2 + slot], chosen_of[slot])] for slot in range(2)
    ]
    ours = [[jnp.where(core == 0, a, b) for a, b in zip(chosen_of[slot], chosen_of[2 + slot])] for slot in range(2)]

    def q_copy(half, slot, way):
        return remote(
            qd.at[y, half, slot],
            qd.at[y, half, slot],
            s_q.at[half, slot, way],
            r_q.at[y, half, slot],
            right if way == 0 else left,
        )

    def st_copy(half, slot, way):
        return remote(
            st.at[y, half, slot],
            st.at[y, half, slot],
            s_st.at[half, slot, way],
            r_st.at[y, half, slot],
            right if way == 0 else left,
        )

    def start_q(half, slot):
        for way in range(2):
            st_copy(half, slot, way).start()
            q_copy(half, slot, way).start()

    sib_copies = [
        remote(kv_sib.at[0], kv.at[0, core], s_sib.at[4], r_sib.at[4], sibling),
    ]
    for slot in range(2):
        sib_copies.append(remote(q_sib.at[slot], qd.at[y, core, slot], s_sib.at[slot], r_sib.at[slot], sibling))
        sib_copies.append(
            remote(st_sib.at[slot], st.at[y, core, slot], s_sib.at[2 + slot], r_sib.at[2 + slot], sibling)
        )

    sib_copies.append(remote(kv_sib.at[1], kv1.at[y * other, core], s_sib.at[5], r_sib.at[5], sibling))

    for slot in range(2):
        pack_keys(theirs[slot], kv_sib.at[slot])
    pack_queries(ours[0], qd.at[y, core, 0], st.at[y, core, 0])
    pl.semaphore_wait(barrier, greetings)
    start_q(core, 0)
    sib_copies[0].start()
    sib_copies[5].start()
    pack_keys(ours[0], kv.at[0, core])
    pack_keys(ours[1], kv1.at[home, core])
    pack_queries(theirs[0], q_sib.at[0], st_sib.at[0])
    sib_copies[1].start()
    sib_copies[2].start()

    def up_copy(d, part):
        return remote(
            kv.at[d, :, part], kv.at[d + 1, :, part], s_up.at[d, part], r_kv.at[d + 1, part], above
        )

    def down_copy(e, part):
        return remote(
            kv.at[(8 - e) % 8, :, part], kv.at[7 - e, :, part], s_down.at[e, part], r_kv.at[7 - e, part], below
        )

    def goes_up(d):
        return (z + 1 < PLANES) & (z >= d) & (d < up_reach)

    def goes_down(e):
        return (core == 0) & (e < DOWN) & ((z + e) % 8 < DOWN)

    def kv_landed(d, part):
        return remote(kv.at[0, :, 0], kv.at[d, :, part], s_up.at[0, 0], r_kv.at[d, part], sibling)

    def hop(i):
        for part in range(2):
            if not isinstance(i, int):

                @pl.when((z >= i) & (i <= up_reach))
                def _(part=part):
                    kv_landed(i, part).wait_recv()

            @pl.when(goes_up(i))
            def _(part=part):
                up_copy(i, part).start()

            if not isinstance(i, int):

                @pl.when((core == 0) & ((z + i) % 8 < DOWN))
                def _(part=part):
                    kv_landed(8 - i, part).wait_recv()

            @pl.when(goes_down(i))
            def _(part=part):
                down_copy(i, part).start()

    def near_copy(j):
        return remote(kv1.at[0], kv1.at[j], s_near.at[j], r_near.at[j], at_chip(chip + j))

    def lift_copy(d):
        return remote(kv1.at[4 * d + y], kv1.at[4 * d + 4 + y], s_near.at[d], r_near.at[4 * d + 4 + y], above)

    def round_copy(d, dy):
        block = 4 * d + y
        return remote(kv1.at[block], kv1.at[block], s_near.at[3 * d + dy + 2], r_near.at[block], at(z, (y + dy) % 4, core))

    def near_landed(block):
        return remote(kv1.at[0], kv1.at[block], s_near.at[0], r_near.at[block], sibling)

    def lifts(d):
        return (core == 1) & (d < 2) & (z >= d) & (z + 1 < PLANES)

    def rounds(d, dy):
        col = (y + dy) % 4
        blocks = 4 * d + col - y
        return (core == 1) & (z >= d) & (blocks >= 0) & (blocks <= REACH[1][1])

    def lift(d):
        if d > 0:

            @pl.when((core == 1) & (z >= d))
            def _():
                near_landed(4 * d + y).wait_recv()

        if d < 2:

            @pl.when(lifts(d))
            def _():
                lift_copy(d).start()

    def start_near():
        for j in range(1, NEAR + 1):

            @pl.when(feeds(j))
            def _(j=j):
                near_copy(j).start()

    def start_rounds():
        for d in range(3):
            for dy in (1, 3, 2):

                @pl.when(rounds(d, dy))
                def _(d=d, dy=dy):
                    round_copy(d, dy).start()

    sib_copies[0].wait_recv()
    hop(0)
    sib_copies[5].wait_recv()
    lift(0)
    start_near()
    pack_queries(theirs[1], q_sib.at[1], st_sib.at[1])
    sib_copies[3].start()
    sib_copies[4].start()
    sib_copies[1].wait_recv()
    sib_copies[2].wait_recv()
    start_q(other, 0)
    pack_queries(ours[1], qd.at[y, core, 1], st.at[y, core, 1])

    dkv_acc[...] = jnp.zeros_like(dkv_acc)
    dkv1_acc[...] = jnp.zeros_like(dkv1_acc)
    own_limits = [jnp.where(core == 0, limits[slot], limits[2 + slot]) for slot in range(2)]

    def tile(slot, col, d0, count, masked, blocks=0):
        size = count * 256
        keys, acc = (kv, dkv_acc) if slot == 0 else (kv1, dkv1_acc)
        into = pl.ds(d0, count)
        k = keys[pl.ds(d0, count), :, 0].reshape(size, HEAD_DIM)
        v = keys[pl.ds(d0, count), :, 1].reshape(size, HEAD_DIM)
        k_t = k.T
        base = d0 * 1024 + (col - y) * 256 if slot == 0 else blocks * 256
        if count == 1:
            groups = [[(half, pair) for half in range(2) for pair in range(2)]]
        else:
            groups = [[(half, pair)] for half in range(2) for pair in range(2)]
        for group in groups:
            width = 256 * len(group)

            def rows(what, group=group, width=width):
                return jnp.concatenate(
                    [
                        qd[col, half, slot, what, 2 * pair : 2 * pair + 2].reshape(256, HEAD_DIM)
                        for half, pair in group
                    ],
                    axis=0,
                )

            def stats(first, group=group):
                return jnp.concatenate(
                    [st[col, half, slot, first + pair : first + pair + 1] for half, pair in group], axis=1
                )

            q, g = rows(0), rows(1)
            prob = jnp.exp2(dot(k, q, NT) * (SCALING * LOG2E) - stats(0))
            if masked:
                key = lax.broadcasted_iota(jnp.int32, (size, width), 0)
                lane = lax.broadcasted_iota(jnp.int32, (size, width), 1)
                row = lane % ROWS + lane // 512 * ROWS
                ahead = row - key
                seen_by = ahead < own_limits[slot] - base
                if masked != "window":
                    seen_by = seen_by & (ahead >= -base)
                prob = jnp.where(seen_by, prob, 0.0)
            ds = (prob * (dot(v, g, NT) - stats(2))).astype(BF16)
            low = prob.astype(BF16)
            acc[0, into] += dot(ds, q).reshape(count, 256, HEAD_DIM)
            acc[1, into] += dot(low, g).reshape(count, 256, HEAD_DIM)
            change = dot(k_t, ds)
            for n, (half, pair) in enumerate(group):
                dq_acc[slot, half, pair] += change[:, n * 256 : (n + 1) * 256]

    def last_block(table, slot, ahead):
        return jnp.minimum(z, (by_class(table, core, slot) - ahead + 4) // 4 - 1)

    def write_dq(col, slot):
        for half in range(2):
            for pair in range(2):
                total = dq_acc[slot, half, pair].T * SCALING
                dq_part[col, slot, half, 2 * pair : 2 * pair + 2] = total.reshape(2, ROWS, HEAD_DIM).astype(BF16)

    def q_landed(col, half, slot):
        return remote(qd.at[0, 0, 0], qd.at[col, half, slot], s_q.at[0, 0, 0], r_q.at[col, half, slot], sibling)

    def st_landed(col, half, slot):
        return remote(st.at[0, 0, 0], st.at[col, half, slot], s_st.at[0, 0, 0], r_st.at[col, half, slot], sibling)

    def q_forward(slot, half):
        col, to = (before, right) if half == 0 else (after, left)
        return (
            remote(
                st.at[col, half, slot], st.at[col, half, slot], s_fst.at[slot, half], r_st.at[col, half, slot], to
            ),
            remote(qd.at[col, half, slot], qd.at[col, half, slot], s_fq.at[slot, half], r_q.at[col, half, slot], to),
        )

    def pass_queries(slot, which):
        for half in range(2):

            @pl.when(which == half)
            def _(half=half):
                col = before if half == 0 else after
                st_landed(col, half, slot).wait_recv()
                q_landed(col, half, slot).wait_recv()
                for c in q_forward(slot, half):
                    c.start()

    def await_queries(slot, dy):
        col = (y + dy) % 4
        for half in range(2):

            @pl.when((dy != 3) if half == 0 else (dy != 1))
            def _(half=half):
                st_landed(col, half, slot).wait_recv()
                q_landed(col, half, slot).wait_recv()

    scales = (SCALING, 1.0)

    def dkv_landed(d):
        return remote(dkv_send.at[0], dkv_in.at[d], s_dkv.at[0], r_dkv.at[d], sibling)

    def dkv_back(d):
        return remote(dkv_send.at[d], dkv_in.at[d], s_dkv.at[d], r_dkv.at[d], at((z + 8 - d) % 8, y, core))

    def dkv_join(d):
        return remote(dkv_send.at[d], dkv_in.at[d], s_dkv.at[d], r_dkv.at[d], at((z + 10 - d) % 8, y, core))

    def ready(d):
        for part in range(2):
            dkv_send[d, part] = (dkv_acc[part, d] * scales[part]).astype(BF16)

    def start_back(d):
        ready(d)
        dkv_back(d).start()

    def first_level():
        @pl.when((core == 1) & (z >= 4))
        def _():
            ready(4)
            dkv_join(4).start()

        @pl.when(z >= 3)
        def _():
            ready(3)
            dkv_join(3).start()

        @pl.when(z >= 1)
        def _():
            start_back(1)

    def second_level():
        @pl.when(z >= 2)
        def _():
            for part in range(2):
                dkv_acc[part, 2] = dkv_acc[part, 2] * scales[part]

            for d in (3, 4):

                @pl.when((z + d - 2 < PLANES) & (core >= d - 3))
                def _(d=d):
                    dkv_landed(d).wait_recv()
                    for part in range(2):
                        dkv_acc[part, 2] = dkv_acc[part, 2] + dkv_in[d, part].astype(F32)

            for part in range(2):
                dkv_send[2, part] = dkv_acc[part, 2].astype(BF16)
            dkv_back(2).start()

    def near_back(j):
        return remote(near_send.at[j], near_in.at[j], s_nback.at[j], r_nback.at[j], at_chip(chip - j))

    def lower_back(d):
        block = 4 * d + y
        return remote(
            near_send.at[block], near_in.at[block], s_nback.at[block], r_nback.at[block], at((z + 8 - d) % 8, y, core)
        )

    def round_back(block):
        entry = block - block % 4 + y
        return remote(
            near_send.at[block], near_in.at[entry], s_nback.at[block], r_nback.at[entry], at(z, block % 4, core)
        )

    def near_back_landed(block):
        return remote(near_send.at[0], near_in.at[block], s_nback.at[0], r_nback.at[block], sibling)

    def place_of(t):
        d, col = 2 - t // 4, t % 4
        block = (1 - core) * t + core * (4 * d + col)
        blocks = (1 - core) * t + core * (4 * d + y - col)
        return d, col, block, blocks

    def middle_sees(d, seer, col):
        blocks = 4 * d + seer - col
        return (core == 1) & (z >= d) & (blocks >= 0) & (blocks <= REACH[1][1])

    def second(t, carry):
        d, col, block, blocks = place_of(t)
        short = (core == 0) & (chip >= blocks)
        middle = (core == 1) & (z >= d) & (blocks >= 0) & (blocks <= REACH[1][1])

        @pl.when(short | middle)
        def _():
            @pl.when(((core == 0) & (blocks > 0)) | ((core == 1) & (col != y)))
            def _():
                near_landed(block).wait_recv()

            plain = (core == 1) & (blocks >= 1) & (blocks <= PLAIN[1][1])

            @pl.when(plain)
            def _():
                tile(1, y, block, 1, False, blocks)

            @pl.when(jnp.logical_not(plain))
            def _():
                tile(1, y, block, 1, True, blocks)

            for part in range(2):
                near_send[block, part] = (dkv1_acc[part, block] * scales[part]).astype(BF16)

            @pl.when((core == 0) & (blocks > 0))
            def _():
                near_back(block).start()

            @pl.when((core == 1) & (col != y))
            def _():
                round_back(block).start()

        return carry

    dq_acc[...] = jnp.zeros_like(dq_acc)
    tile(0, y, 0, 1, True)

    def step(i, carry):
        @pl.when(i == 3)
        def _():
            pass_queries(0, core)

        @pl.when(i == 4)
        def _():
            pass_queries(0, other)

        hop(i)

        @pl.when(i == 1)
        def _():
            sib_copies[3].wait_recv()
            sib_copies[4].wait_recv()

        @pl.when(i == 2)
        def _():
            lift(1)

        @pl.when(i == 3)
        def _():
            lift(2)

        @pl.when(i == 4)
        def _():
            start_rounds()

        full, end = last_block(PLAIN, 0, 0), last_block(REACH, 0, 0)
        here = (i <= up_reach) & (i <= end)

        @pl.when(here & (i <= full))
        def _():
            tile(0, y, i, 1, False)

        @pl.when(here & (i > full))
        def _():
            tile(0, y, i, 1, "window")

        @pl.when((core == 0) & (z >= 8 - i))
        def _():
            tile(0, y, 8 - i, 1, False)

        @pl.when(i < 4)
        def _():
            second((1 - core) * (i - 1) + core * (4 * (3 - i) + y), 0)

        return carry

    lax.fori_loop(1, 5, step, 0)
    write_dq(y, 0)

    def dq_copy(dy):
        col = (y + dy) % 4
        return remote(dq_part.at[col, 0], dq_in.at[y], s_dq.at[dy], r_dq.at[y], at(z, col, core))

    def join(d):
        @pl.when(core == 1)
        def _():
            for part in range(2):
                dkv1_acc[part, 4 * d + y] = dkv1_acc[part, 4 * d + y] * scales[part]

        for dy in range(1, COLUMNS):
            col = (y + dy) % 4

            @pl.when(middle_sees(d, col, y))
            def _(col=col):
                near_back_landed(4 * d + col).wait_recv()
                for part in range(2):
                    dkv1_acc[part, 4 * d + y] = dkv1_acc[part, 4 * d + y] + near_in[4 * d + col, part].astype(F32)

        if d > 0:

            @pl.when((core == 1) & (z >= d))
            def _():
                for part in range(2):
                    near_send[4 * d + y, part] = dkv1_acc[part, 4 * d + y].astype(BF16)
                lower_back(d).start()

    def nth(n):
        return n + (n // 2) * (1 - 2 * (n % 2))

    def one_column(n):
        dy = nth(n)
        col = (y + dy) % 4
        ahead = col - y
        await_queries(0, dy)
        dq_acc[0] = jnp.zeros_like(dq_acc[0])
        first = jnp.where(ahead > 0, 0, 1)
        full, end = last_block(PLAIN, 0, ahead), last_block(REACH, 0, ahead)
        large = (core == 0) & (z >= 3)
        below_count = jnp.where(large, 1 - first, jnp.maximum(full - first + 1, 0))
        above_count = jnp.where(large & (z < 7), z - 3, 0)

        @pl.when(large & (z == 7))
        def _():
            tile(0, col, 4, 4, False)

            @pl.when(n == 3)
            def _():
                for d in range(4, PLANES):
                    start_back(d)

        def plain(m, cc):
            d = jnp.where(m < below_count, first + m, 4 + m - below_count)
            tile(0, col, d, 1, False)
            return cc

        lax.fori_loop(0, below_count + above_count, plain, 0)

        def masked(d, cc):
            tile(0, col, d, 1, "window")
            return cc

        lax.fori_loop(jnp.maximum(full + 1, first), end + 1, masked, 0)

        @pl.when(large)
        def _():
            tile(0, col, 1, 3, False)

        write_dq(col, 0)
        dq_copy(dy).start()


    def phase(n, carry):
        one_column(n)

        @pl.when(n == 3)
        def _():
            first_level()

            def rest_back(d, cc):
                start_back(d)
                return cc

            lax.fori_loop(4, jnp.where((core == 0) & (z < 7), z + 1, 4), rest_back, 0)

        return carry

    lax.fori_loop(1, COLUMNS, phase, 0)

    def slot_one(t, carry):
        @pl.when(t == 8)
        def _():
            second_level()
            join(2)

        @pl.when(t % 4 != y)
        def _():
            second(t, 0)

        return carry

    lax.fori_loop(0, 12 * core, slot_one, 0)
    join(1)

    @pl.when(core == 0)
    def _():
        second_level()

    write_dq(y, 1)
    join(0)

    def fin(ref, slot, n):
        return remote(ref.at[0, slot], ref.at[2, slot], s_fin.at[n, slot], r_fin.at[n, slot], sibling)

    for part_half in range(2):
        half = core if part_half == 1 else other
        for g in range(GROUP):
            fq[part_half, 1, g] = dq_part[y, 1, half, g]
    fin(fq, 1, 0).start()
    for dy in range(1, COLUMNS):
        col = (y + dy) % 4
        remote(dq_part.at[0, 0], dq_in.at[col], s_dq.at[0], r_dq.at[col], sibling).wait_recv()
    for part_half in range(2):
        half = core if part_half == 1 else other
        for g in range(GROUP):
            total = dq_part[y, 0, half, g].astype(F32)
            for dy in range(1, COLUMNS):
                total += dq_in[(y + dy) % 4, half, g].astype(F32)
            fq[part_half, 0, g] = total.astype(BF16)
    fin(fq, 0, 0).start()

    def add_near(block):
        near_back_landed(block).wait_recv()
        for part in range(2):
            dkv1_acc[part, home] = dkv1_acc[part, home] + near_in[block, part].astype(F32)

    @pl.when(core == 0)
    def _():
        dkv1_acc[0, 0] = dkv1_acc[0, 0] * SCALING

    for j in range(1, NEAR + 1):

        @pl.when(feeds(j))
        def _(j=j):
            add_near(j)

    for d in (1, 2):

        @pl.when((core == 1) & (z + d < PLANES))
        def _(d=d):
            add_near(4 * d + y)

    dkv_acc[0, 0] = dkv_acc[0, 0] * SCALING

    for d in (1, 2, 4, 5, 6, 7):

        @pl.when((z + d < PLANES) & ((core == 0) | (d < 3)))
        def _(d=d):
            dkv_landed(d).wait_recv()
            for part in range(2):
                dkv_acc[part, 0] = dkv_acc[part, 0] + dkv_in[d, part].astype(F32)

    for slot in range(2):
        for part in range(2):
            for part_half in range(2):
                half = core if part_half == 1 else other
                rows = pl.ds(pl.multiple_of(half * ROWS, ROWS), ROWS)
                acc, entry = (dkv_acc, 0) if slot == 0 else (dkv1_acc, home)
                fkv[part_half, slot, part] = acc[part, entry, rows].astype(BF16)
        fin(fkv, slot, 1).start()
    for slot in range(2):
        fin(fq, slot, 0).wait_recv()

    def entry(kind):
        return 1 + (core + kind // 2) % 2

    def place_head(head, what):
        masks = [jnp.full((ROWS, HEAD_DIM), chosen_of[kind][head], jnp.int32) > 0 for kind in range(4)]

        def picked(read):
            total = jnp.zeros((ROWS, HEAD_DIM), F32)
            for kind in range(4):
                total = jnp.where(masks[kind], read(entry(kind), kind % 2).astype(F32), total)
            return total.astype(BF16)

        if what == 0:
            for g in range(GROUP):
                cols = slice((head * GROUP + g) * HEAD_DIM, (head * GROUP + g + 1) * HEAD_DIM)
                dq_out[:, cols] = picked(lambda e, slot, g=g: fq[e, slot, g])
        else:
            cols = slice(head * HEAD_DIM, (head + 1) * HEAD_DIM)
            dk_out[:, cols] = picked(lambda e, slot: fkv[e, slot, 0])
            dv_out[:, cols] = picked(lambda e, slot: fkv[e, slot, 1])

    for head in range(KV_HEADS):
        place_head(head, 0)
    for slot in range(2):
        fin(fkv, slot, 1).wait_recv()
    for head in range(KV_HEADS):
        place_head(head, 1)

    for c in sib_copies:
        c.wait_send()
    for slot in range(2):
        fin(fq, slot, 0).wait_send()
        fin(fkv, slot, 1).wait_send()
    for half in range(2):
        for c in q_forward(0, half):
            c.wait_send()
        for way in range(2):
            st_copy(half, 0, way).wait_send()
            q_copy(half, 0, way).wait_send()
    for dy in range(1, COLUMNS):
        dq_copy(dy).wait_send()

    def sent(i, carry):
        for part in range(2):

            @pl.when(goes_up(i))
            def _(part=part):
                up_copy(i, part).wait_send()

            @pl.when(goes_down(i))
            def _(part=part):
                down_copy(i, part).wait_send()

        return carry

    lax.fori_loop(0, 5, sent, 0)

    for d in range(1, PLANES):

        @pl.when((z >= d) & ((core == 0) | (d <= UP[1])))
        def _(d=d):
            dkv_back(d).wait_send()

    for j in range(1, NEAR + 1):

        @pl.when(feeds(j))
        def _(j=j):
            near_copy(j).wait_send()

    for d in range(3):

        @pl.when(lifts(d))
        def _(d=d):
            lift_copy(d).wait_send()

        for dy in range(1, COLUMNS):

            @pl.when(rounds(d, dy))
            def _(d=d, dy=dy):
                round_copy(d, dy).wait_send()

            col = (y + dy) % 4

            @pl.when(middle_sees(d, y, col))
            def _(d=d, col=col):
                round_back(4 * d + col).wait_send()

        if d > 0:

            @pl.when((core == 1) & (z >= d))
            def _(d=d):
                lower_back(d).wait_send()

    for j in range(1, NEAR + 1):

        @pl.when(fed_by(j))
        def _(j=j):
            near_back(j).wait_send()


def per_device(queries, keys, values, outputs, out_grad, log_sum_exp, spans):
    whole = pl.BlockSpec(memory_space=pltpu.VMEM)
    dma = pltpu.SemaphoreType.DMA
    near_count = 3 * COLUMNS
    return tuple(
        pl.pallas_call(
            kernel,
            in_specs=[pl.BlockSpec(memory_space=pltpu.SMEM)] + [whole] * 6,
            out_specs=[whole] * 3,
            out_shape=[
                jax.ShapeDtypeStruct((ROWS, Q_HEADS * HEAD_DIM), BF16),
                jax.ShapeDtypeStruct((ROWS, KV_HEADS * HEAD_DIM), BF16),
                jax.ShapeDtypeStruct((ROWS, KV_HEADS * HEAD_DIM), BF16),
            ],
            scratch_shapes=[
                pltpu.VMEM((COLUMNS, 2, 2, 2, GROUP, ROWS, HEAD_DIM), BF16),
                pltpu.VMEM((PLANES, 2, 2, ROWS, HEAD_DIM), BF16),
                pltpu.VMEM((near_count, 2, 2, ROWS, HEAD_DIM), BF16),
                pltpu.VMEM((COLUMNS, 2, 2, 8, 256), F32),
                pltpu.VMEM((2, 2, GROUP, ROWS, HEAD_DIM), BF16),
                pltpu.VMEM((2, 2, ROWS, HEAD_DIM), BF16),
                pltpu.VMEM((2, 8, 256), F32),
                pltpu.VMEM((2, 2, 2, HEAD_DIM, 256), F32),
                pltpu.VMEM((2, PLANES, 256, HEAD_DIM), F32),
                pltpu.VMEM((2, near_count, 256, HEAD_DIM), F32),
                pltpu.VMEM((COLUMNS, 2, 2, GROUP, ROWS, HEAD_DIM), BF16),
                pltpu.VMEM((COLUMNS, 2, GROUP, ROWS, HEAD_DIM), BF16),
                pltpu.VMEM((PLANES, 2, 256, HEAD_DIM), BF16),
                pltpu.VMEM((PLANES, 2, 256, HEAD_DIM), BF16),
                pltpu.VMEM((near_count, 2, 256, HEAD_DIM), BF16),
                pltpu.VMEM((near_count, 2, 256, HEAD_DIM), BF16),
                pltpu.VMEM((3, 2, GROUP, ROWS, HEAD_DIM), BF16),
                pltpu.VMEM((3, 2, 2, ROWS, HEAD_DIM), BF16),
                dma((6,)),
                dma((6,)),
                dma((2, 2, 2)),
                dma((2, 2, 2)),
                dma((COLUMNS, 2, 2)),
                dma((COLUMNS, 2, 2)),
                dma((2, 2)),
                dma((2, 2)),
                dma((PLANES, 2)),
                dma((PLANES, 2)),
                dma((PLANES, 2)),
                dma((near_count,)),
                dma((near_count,)),
                dma((COLUMNS,)),
                dma((COLUMNS,)),
                dma((PLANES,)),
                dma((PLANES,)),
                dma((near_count,)),
                dma((near_count,)),
                dma((2, 2)),
                dma((2, 2)),
            ],
            compiler_params=pltpu.CompilerParams(
                collective_id=0, has_side_effects=True, vmem_limit_bytes=56 * 2**20
            ),
            name="gradients",
        )(spans, queries, keys, values, outputs, out_grad, log_sum_exp)
    )


def solution(mesh):
    in_specs = (
        P(("dp", "ctx"), None),
        P(("dp", "ctx"), None),
        P(("dp", "ctx"), None),
        P(("dp", "ctx"), None),
        P(("dp", "ctx"), None),
        P(None, ("dp", "ctx")),
        P("dp"),
    )
    out_specs = (P(("dp", "ctx"), None), P(("dp", "ctx"), None), P(("dp", "ctx"), None))
    return jax.shard_map(
        per_device, mesh=mesh, in_specs=in_specs, out_specs=out_specs, check_vma=False
    )
```
